32 devices in a mesh: grp: 4 (over x, core), row: 8 (over z, y).
Axes of the slice: x: 2, y: 2, z: 4, core: 2. Of those that a mesh axis runs over, the one named last changes fastest.
Arguments:
- pixels: bfloat16 [4, 8, 128, 202, 256], P('grp', 'row'), may hold values from -6 to 6
- wave_table: float32 [256], replicated, may hold values from 0.4 to 2.5
- wave_weight: bfloat16 [128, 128], replicated, may hold values from -0.5 to 0.5
- wave_bias: float32 [128], replicated, may hold values from -3 to 3
- gen_weight: bfloat16 [32768, 768], P('row'), may hold values from -0.01171875 to 0.01171875
- patch_bias: float32 [768], replicated, may hold values from -2 to 2
- norm1_gain: float32 [768], replicated, may hold values from 0.5 to 1.5
- norm1_bias: float32 [768], replicated, may hold values from -2 to 2
- qkv_weight: bfloat16 [768, 2304], P('row'), may hold values from -0.21875 to 0.21875
- query_bias: float32 [768], replicated, may hold values from -2 to 2
- value_bias: float32 [768], replicated, may hold values from -2 to 2
- out_weight: bfloat16 [768, 768], P('row'), may hold values from -0.875 to 0.875
- out_bias: float32 [768], replicated, may hold values from -2 to 2
- norm2_gain: float32 [768], replicated, may hold values from 0.5 to 1.5
- norm2_bias: float32 [768], replicated, may hold values from -2 to 2
- fc1_weight: bfloat16 [768, 3072], P('row'), may hold values from -0.21875 to 0.21875
- fc1_bias: float32 [3072], replicated, may hold values from -2 to 2
- fc2_weight: bfloat16 [3072, 768], P('row'), may hold values from -0.109375 to 0.109375
- fc2_bias: float32 [768], replicated, may hold values from -2 to 2
- band_count: int32 [4], P('grp'), may hold values from 2 to 202, as said below
- band_table: int32 [4, 202], P('grp'), may hold values from 0 to 255
- cotangent: bfloat16 [4, 8, 128, 768], P('grp', 'row'), may hold values from -6 to 6
Outputs:
- block_out: bfloat16 [4, 8, 128, 768], P('grp', 'row')
- pixel_grad: bfloat16 [4, 8, 128, 202, 256], P('grp', 'row')
- wave_weight_grad: float32 [128, 128], replicated
- wave_bias_grad: float32 [128], replicated
- gen_weight_grad: float32 [32768, 768], P('row')
- patch_bias_grad: float32 [768], replicated
- norm1_gain_grad: float32 [768], replicated
- norm1_bias_grad: float32 [768], replicated
- qkv_weight_grad: float32 [768, 2304], P('row')
- query_bias_grad: float32 [768], replicated
- value_bias_grad: float32 [768], replicated
- out_weight_grad: float32 [768, 768], P('row')
- out_bias_grad: float32 [768], replicated
- norm2_gain_grad: float32 [768], replicated
- norm2_bias_grad: float32 [768], replicated
- fc1_weight_grad: float32 [768, 3072], P('row')
- fc1_bias_grad: float32 [3072], replicated
- fc2_weight_grad: float32 [3072, 768], P('row')
- fc2_bias_grad: float32 [768], replicated
The draws below stay inside these ranges and needn't reach their ends.
Inputs may be any that keep to these rules, and one draw needn't show every extreme that they name: `band_count`: each group's number of live band slots; some group uses all 202. `band_table`: entries of wave_table.
All inputs are finite; a program needn't handle non-finite values.
Results may differ from the reference program's by a relative error of at most 0.019.
Values may be sent and summed in bfloat16 or wider, within the bound.
No kernel may reach another device: no remote copies, remote signals or barrier semaphores. Data moves between devices by JAX's collectives and lax.ppermute only.
A program may use at most 384 MiB of HBM per device.

```python
import math
import jax
import jax.numpy as jnp
from jax import lax

D = 768
HEADS = 12
FF = 3072
WV = 128
PIX = 256
SEQ = 128
BSLOT = 202
WTAB = 256
GROUPS = 4
TILES = 8


def draw_band_count(key, part):
    key = jax.random.fold_in(key, 7)
    first_key, second_key = jax.random.split(key)
    counts = jax.random.randint(first_key, (GROUPS,), 2, BSLOT + 1)
    chosen = jax.random.randint(second_key, (), 0, GROUPS)
    return jnp.where(jnp.arange(GROUPS) == chosen, BSLOT, counts).astype(jnp.int32)


def touch_ends(entries, stream_key, least, largest):
    dims = entries.shape
    place = [jax.random.randint(jax.random.fold_in(stream_key, axis), (), 0, dims[axis]) for axis in range(len(dims))]
    entries = entries.at[tuple(place)].set(least)
    longest = dims.index(max(dims))
    place[longest] = (place[longest] + 1) % dims[longest]
    return entries.at[tuple(place)].set(largest)


def shard_levels(rng, shape, cuts, least, largest):
    level = 1.0
    for axis_at, parts in cuts:
        heights = jax.random.uniform(jax.random.fold_in(jax.random.fold_in(rng, 6), axis_at), (parts,), jnp.float32, least / len(cuts), largest / len(cuts))
        level = level * jnp.repeat(jnp.exp(heights), shape[axis_at] // parts).reshape((-1,) + (1,) * (len(shape) - 1 - axis_at))
    return level


def scatter_about(own_key, shape, deviation, limit, cuts=(), held_as=jnp.bfloat16):
    loudness = shard_levels(own_key, shape, cuts, -0.22, 0.18) if cuts else 1.0
    values = jax.random.normal(own_key, shape, jnp.float32) * deviation * loudness
    return jnp.minimum(jnp.maximum(values, -limit), limit).astype(held_as)


def setup_inputs(seed: int = 0) -> dict:
    splits = jax.random.split(jax.random.key(seed), 23)
    return {
        "pixels": scatter_about(splits[0], (GROUPS, TILES, SEQ, BSLOT, PIX), 1.0, 6.0, ((0, 4), (1, 8))),
        "wave_table": jnp.clip(jnp.exp(jax.random.uniform(splits[1], (WTAB,), jnp.float32, math.log(0.4), math.log(2.5))), 0.4, 2.5),
        "wave_weight": scatter_about(splits[2], (WV, WV), WV ** -0.5, 0.5),
        "wave_bias": scatter_about(splits[3], (WV,), 0.5, 3.0, (), jnp.float32),
        "gen_weight": scatter_about(splits[4], (WV * PIX, D), (WV * PIX * 8) ** -0.5, 0.01171875, ((0, 8),)),
        "patch_bias": scatter_about(splits[5], (D,), 0.3, 2.0, (), jnp.float32),
        "norm1_gain": jnp.clip(1.0 + 0.1 * jax.random.normal(splits[6], (D,), jnp.float32), 0.5, 1.5),
        "norm1_bias": scatter_about(splits[7], (D,), 0.3, 2.0, (), jnp.float32),
        "qkv_weight": scatter_about(splits[8], (D, 3 * D), D ** -0.5, 0.21875, ((0, 8),)),
        "query_bias": scatter_about(splits[9], (D,), 0.3, 2.0, (), jnp.float32),
        "value_bias": scatter_about(splits[10], (D,), 0.3, 2.0, (), jnp.float32),
        "out_weight": scatter_about(splits[11], (D, D), (D // 16) ** -0.5, 0.875, ((0, 8),)),
        "out_bias": scatter_about(splits[12], (D,), 0.3, 2.0, (), jnp.float32),
        "norm2_gain": jnp.clip(1.0 + 0.1 * jax.random.normal(splits[13], (D,), jnp.float32), 0.5, 1.5),
        "norm2_bias": scatter_about(splits[14], (D,), 0.3, 2.0, (), jnp.float32),
        "fc1_weight": scatter_about(splits[15], (D, FF), D ** -0.5, 0.21875, ((0, 8),)),
        "fc1_bias": scatter_about(splits[16], (FF,), 0.3, 2.0, (), jnp.float32),
        "fc2_weight": scatter_about(splits[17], (FF, D), FF ** -0.5, 0.109375, ((0, 8),)),
        "fc2_bias": scatter_about(splits[18], (D,), 0.3, 2.0, (), jnp.float32),
        "band_count": draw_band_count(jax.random.fold_in(splits[22], 71), 0),
        "band_table": touch_ends(jax.random.randint(splits[20], (GROUPS, BSLOT), 0, WTAB), jax.random.fold_in(splits[20], 1), 0, WTAB - 1).astype(jnp.int32),
        "cotangent": scatter_about(splits[21], (GROUPS, TILES, SEQ, D), 1.0, 6.0, ((0, 4), (1, 8))),
    }


@jax.custom_vjp
def low(v):
    return lax.optimization_barrier(v.astype(jnp.bfloat16)).astype(jnp.float32)

@jax.custom_vjp
def low_back(v):
    return v

def low_keep(v):
    return (low(v), None)

def low_pass(kept, grad):
    return (grad,)

def back_keep(v):
    return (v, None)

def back_low(kept, grad):
    return (low(grad),)
low.defvjp(low_keep, low_pass)
low_back.defvjp(back_keep, back_low)
highest = lax.Precision.HIGHEST
epsilon = 1e-06

def sincos(angles_in, out_width):
    half_width = out_width // 2
    freqs = 1.0 / 10000.0 ** (jnp.arange(half_width).astype(angles_in.dtype) * (2.0 / out_width))
    angles = angles_in[:, None] * freqs[None, :]
    return jnp.concatenate([jnp.sin(angles), jnp.cos(angles)], axis=1)

def layer_norm(inputs, gain, shift):
    center = inputs - lax.optimization_barrier(jnp.mean(inputs, axis=-1, keepdims=True))
    spread = lax.optimization_barrier(jnp.mean(center * center, axis=-1, keepdims=True))
    return center * lax.rsqrt(spread + epsilon) * gain + shift

def matmul(left, right):
    return jnp.dot(left, right, precision=highest, preferred_element_type=jnp.float32)

def reference(pixels, wave_table, wave_weight, wave_bias, gen_weight, patch_bias, norm1_gain, norm1_bias, qkv_weight, query_bias, value_bias, out_weight, out_bias, norm2_gain, norm2_bias, fc1_weight, fc1_bias, fc2_weight, fc2_bias, band_count, band_table, cotangent):
    group_total, tile_count, seq_len, band_slots, pixel_count = pixels.shape
    model_width = gen_weight.shape[1]
    wave_width = wave_weight.shape[0]
    head_size = model_width // HEADS
    score_scale = head_size ** (-0.5)
    wavelength = wave_table.astype(jnp.float32)[band_table.reshape(-1)]
    wave_embed = sincos(wavelength * 1000.0, wave_width).reshape(group_total, band_slots, wave_width)
    live = (jnp.arange(band_slots)[None, :] < band_count[:, None]).astype(jnp.float32)[:, :, None]
    position = sincos(jnp.arange(seq_len).astype(jnp.float32), model_width)
    group_of = jnp.repeat(jnp.arange(group_total, dtype=jnp.int32), tile_count)

    def forward(pixel_all, w_wave, b_wave, w_gen, b_patch, gain_one, shift_one, w_qkv, b_query, b_value, w_out, b_out, gain_two, shift_two, w_fc1, b_fc1, w_fc2, b_fc2):
        hyper = low(jax.nn.gelu(jnp.einsum('gbi,ij->gbj', wave_embed, w_wave, precision=highest) + b_wave) * live)

        def one_tile(tile_args):
            tile_pixels, group_id = tile_args
            hyper_tile = lax.dynamic_index_in_dim(hyper, group_id, 0, keepdims=False)
            patches = jnp.einsum('bk,sbp->skp', hyper_tile, tile_pixels, precision=highest)
            patches = low_back(low(patches.reshape(seq_len, wave_width * pixel_count)))
            embedded = low_back(matmul(patches, w_gen) + b_patch + position)
            normed = low(layer_norm(embedded, gain_one, shift_one))
            mixed = matmul(normed, w_qkv)
            queries = low(low_back(mixed[:, :model_width] + b_query)).reshape(seq_len, HEADS, head_size)
            key_rows = low(low_back(mixed[:, model_width:2 * model_width])).reshape(seq_len, HEADS, head_size)
            value_rows = low(low_back(mixed[:, 2 * model_width:] + b_value)).reshape(seq_len, HEADS, head_size)
            scores = low_back(jnp.einsum('qhd,khd->hqk', queries, key_rows, precision=highest) * score_scale)
            probs = low(jax.nn.softmax(scores, axis=-1))
            attended = jnp.einsum('hqk,khd->qhd', probs, value_rows, precision=highest).reshape(seq_len, model_width)
            attended = low(low_back(attended))
            middle = embedded + low_back(matmul(attended, w_out) + b_out)
            normed_two = low(layer_norm(middle, gain_two, shift_two))
            fc_pre = low_back(matmul(normed_two, w_fc1) + b_fc1)
            hidden = low(jax.nn.gelu(fc_pre))
            return middle + low_back(matmul(hidden, w_fc2) + b_fc2)
        return lax.map(jax.checkpoint(one_tile), (pixel_all, group_of))
    inputs = (pixels.reshape(group_total * tile_count, seq_len, band_slots, pixel_count), wave_weight, wave_bias, gen_weight, patch_bias, norm1_gain, norm1_bias, qkv_weight, query_bias, value_bias, out_weight, out_bias, norm2_gain, norm2_bias, fc1_weight, fc1_bias, fc2_weight, fc2_bias)
    inputs = tuple((item.astype(jnp.float32) for item in inputs))
    result, pullback = jax.vjp(forward, *inputs)
    grads = pullback(cotangent.astype(jnp.float32).reshape(result.shape))
    block_out = result.reshape(group_total, tile_count, seq_len, model_width).astype(jnp.bfloat16)
    pixel_grad = grads[0].reshape(pixels.shape).astype(jnp.bfloat16)
    return (block_out, pixel_grad, grads[1], grads[2], grads[3], grads[4], grads[5], grads[6], grads[7], grads[8], grads[9], grads[10], grads[11], grads[12], grads[13], grads[14], grads[15], grads[16], grads[17])
```

```python
import jax
import jax.numpy as jnp
from jax import lax
from jax.experimental import pallas as pl
from jax.experimental.pallas import tpu as pltpu
from jax.sharding import Mesh
from jax.sharding import PartitionSpec as P

HEADS = 12

bf16 = jnp.bfloat16
f32 = jnp.float32
highest = lax.Precision.HIGHEST
epsilon = 1e-06

AXES = ("x", "c", "z", "y")
VMEM_LIMIT = 48 * 1024 * 1024
MIX_ROWS = 16
GEN_STEP = 4


def sincos(angles_in, out_width):
    half_width = out_width // 2
    freqs = 1.0 / 10000.0 ** (jnp.arange(half_width).astype(angles_in.dtype) * (2.0 / out_width))
    angles = angles_in[:, None] * freqs[None, :]
    return jnp.concatenate([jnp.sin(angles), jnp.cos(angles)], axis=1)


def layer_norm(inputs, gain, shift):
    center = inputs - jnp.mean(inputs, axis=-1, keepdims=True)
    spread = jnp.mean(center * center, axis=-1, keepdims=True)
    return center * lax.rsqrt(spread + epsilon) * gain + shift


def dense_dot(left, right):
    return jnp.dot(left, right, preferred_element_type=f32)


def left_dot(left, right):
    return lax.dot_general(left, right, (((0,), (0,)), ((), ())), preferred_element_type=f32)


def right_dot(left, right):
    return lax.dot_general(left, right, (((1,), (1,)), ((), ())), preferred_element_type=f32)


def row_total(values):
    return jnp.sum(values.astype(f32), axis=0)


def mix_kernel(hyper_ref, pix_ref, out_a, out_b, out_c, out_d, scratch):
    rows = pix_ref.shape[0]
    entries = hyper_ref.shape[0]
    half = pix_ref.shape[2] // 2
    for r in range(rows):
        mixed = dense_dot(hyper_ref[...], pix_ref[r])
        for h in range(2):
            scratch[h, pl.ds(r, entries, stride=rows), :] = mixed[:, h * half : (h + 1) * half]
    for j, out in enumerate((out_a, out_b, out_c, out_d)):
        share = out.shape[0]
        for h in range(2):
            part = scratch[h, j * share * rows : (j + 1) * share * rows, :]
            out[:, :, h * half : (h + 1) * half] = part.reshape(share, rows, half).astype(bf16)


def mix_pixels(hyper_t, pixel_rows):
    entries = hyper_t.shape[0]
    row_count, slots, pixel_count = pixel_rows.shape
    share = entries // 4
    out = jax.ShapeDtypeStruct((share, row_count, pixel_count), bf16)
    return pl.pallas_call(
        mix_kernel,
        grid=(row_count // MIX_ROWS,),
        in_specs=[
            pl.BlockSpec((entries, slots), lambda i: (0, 0)),
            pl.BlockSpec((MIX_ROWS, slots, pixel_count), lambda i: (i, 0, 0)),
        ],
        out_specs=[pl.BlockSpec((share, MIX_ROWS, pixel_count), lambda i: (0, i, 0))] * 4,
        out_shape=[out] * 4,
        scratch_shapes=[pltpu.VMEM((2, entries * MIX_ROWS, pixel_count // 2), f32)],
        compiler_params=pltpu.CompilerParams(vmem_limit_bytes=VMEM_LIMIT),
        cost_estimate=pl.CostEstimate(
            flops=2 * row_count * slots * pixel_count * entries,
            bytes_accessed=2 * row_count * pixel_count * (slots + entries),
            transcendentals=0,
        ),
        name="mix_pixels",
    )(hyper_t, pixel_rows)


def halves(steps):
    first = lambda i: (jnp.minimum(i, steps - 1), 0, 0)
    second = lambda i: (jnp.maximum(i - steps, 0), 0, 0)
    return first, second


def project_kernel(a0, a1, a2, a3, w0, w1, out):
    i = pl.program_id(0)
    steps = pl.num_programs(0) // 2
    rows = a0.shape[1]

    @pl.when(i == 0)
    def _():
        out[...] = jnp.zeros_like(out)

    def add(w):
        for k in range(w.shape[0]):
            left = jnp.concatenate([a[k] for a in (a0, a1, a2, a3)], axis=0)
            out[...] += dense_dot(left, w[k])

    @pl.when(i < steps)
    def _():
        add(w0)

    @pl.when(i >= steps)
    def _():
        add(w1)


def project(parts, near, far):
    share, rows, pixel_count = parts[0].shape
    width = near.shape[2]
    steps = share // 2 // GEN_STEP
    first, second = halves(steps)
    return pl.pallas_call(
        project_kernel,
        grid=(2 * steps,),
        in_specs=[pl.BlockSpec((GEN_STEP, rows, pixel_count), lambda i: (i, 0, 0))] * 4
        + [
            pl.BlockSpec((GEN_STEP, pixel_count, width), first),
            pl.BlockSpec((GEN_STEP, pixel_count, width), second),
        ],
        out_specs=pl.BlockSpec((4 * rows, width), lambda i: (0, 0)),
        out_shape=jax.ShapeDtypeStruct((4 * rows, width), f32),
        compiler_params=pltpu.CompilerParams(vmem_limit_bytes=VMEM_LIMIT),
        cost_estimate=pl.CostEstimate(
            flops=8 * share * rows * pixel_count * width,
            bytes_accessed=2 * share * pixel_count * (4 * rows + width),
            transcendentals=0,
        ),
        name="project",
    )(*parts, near, far)


def back_kernel(g, w0, w1, o0, o1, o2, o3):
    i = pl.program_id(0)
    steps = pl.num_programs(0) // 2
    rows = o0.shape[1]

    def work(w):
        for k in range(w.shape[0]):
            res = right_dot(g[...], w[k]).astype(bf16)
            for j, out in enumerate((o0, o1, o2, o3)):
                out[k] = res[j * rows : (j + 1) * rows]

    @pl.when(i < steps)
    def _():
        work(w0)

    @pl.when(i >= steps)
    def _():
        work(w1)


def back_patches(grads, near, far):
    share, pixel_count, width = 2 * near.shape[0], near.shape[1], near.shape[2]
    rows = grads.shape[0] // 4
    steps = share // 2 // GEN_STEP
    first, second = halves(steps)
    out = jax.ShapeDtypeStruct((share, rows, pixel_count), bf16)
    return pl.pallas_call(
        back_kernel,
        grid=(2 * steps,),
        in_specs=[
            pl.BlockSpec((4 * rows, width), lambda i: (0, 0)),
            pl.BlockSpec((GEN_STEP, pixel_count, width), first),
            pl.BlockSpec((GEN_STEP, pixel_count, width), second),
        ],
        out_specs=[pl.BlockSpec((GEN_STEP, rows, pixel_count), lambda i: (i, 0, 0))] * 4,
        out_shape=[out] * 4,
        compiler_params=pltpu.CompilerParams(vmem_limit_bytes=VMEM_LIMIT),
        cost_estimate=pl.CostEstimate(
            flops=8 * share * rows * pixel_count * width,
            bytes_accessed=2 * share * pixel_count * (4 * rows + width),
            transcendentals=0,
        ),
        name="back_patches",
    )(grads, near, far)


def gen_grad_kernel(a0, a1, a2, a3, g, out):
    for k in range(out.shape[0]):
        left = jnp.concatenate([a[k] for a in (a0, a1, a2, a3)], axis=0)
        out[k] = left_dot(left, g[...]).astype(bf16)


def gen_grad(parts, grads, which):
    share, rows, pixel_count = parts[0].shape
    width = grads.shape[1]
    steps = share // 2 // GEN_STEP
    return pl.pallas_call(
        gen_grad_kernel,
        grid=(steps,),
        in_specs=[pl.BlockSpec((GEN_STEP, rows, pixel_count), lambda i: (i + which * steps, 0, 0))] * 4
        + [pl.BlockSpec((4 * rows, width), lambda i: (0, 0))],
        out_specs=pl.BlockSpec((GEN_STEP, pixel_count, width), lambda i: (i, 0, 0)),
        out_shape=jax.ShapeDtypeStruct((share // 2, pixel_count, width), bf16),
        compiler_params=pltpu.CompilerParams(vmem_limit_bytes=VMEM_LIMIT),
        cost_estimate=pl.CostEstimate(
            flops=4 * share * rows * pixel_count * width,
            bytes_accessed=share * pixel_count * (4 * rows + width),
            transcendentals=0,
        ),
        name="gen_grad",
    )(*parts, grads)


def pixel_kernel(hyper_ref, pix_ref, g0, g1, g2, g3, grad_ref, total_ref, scratch):
    rows = pix_ref.shape[0]
    entries = hyper_ref.shape[1]
    half = pix_ref.shape[2] // 2

    @pl.when(pl.program_id(0) == 0)
    def _():
        total_ref[...] = jnp.zeros_like(total_ref)

    for j, g in enumerate((g0, g1, g2, g3)):
        share = g.shape[0]
        for h in range(2):
            part = g[:, :, h * half : (h + 1) * half].astype(f32)
            scratch[h, j * share * rows : (j + 1) * share * rows, :] = part.reshape(share * rows, half)
    total = total_ref[...]
    for r in range(rows):
        grad = jnp.concatenate(
            [scratch[h, pl.ds(r, entries, stride=rows), :] for h in range(2)], axis=1
        ).astype(bf16)
        grad_ref[r] = dense_dot(hyper_ref[...], grad).astype(bf16)
        total = total + right_dot(pix_ref[r], grad)
    total_ref[...] = total


def pixel_back(hyper, pixel_rows, parts):
    slots, entries = hyper.shape
    row_count, _, pixel_count = pixel_rows.shape
    share = entries // 4
    return pl.pallas_call(
        pixel_kernel,
        grid=(row_count // MIX_ROWS,),
        in_specs=[
            pl.BlockSpec((slots, entries), lambda i: (0, 0)),
            pl.BlockSpec((MIX_ROWS, slots, pixel_count), lambda i: (i, 0, 0)),
        ]
        + [pl.BlockSpec((share, MIX_ROWS, pixel_count), lambda i: (0, i, 0))] * 4,
        out_specs=[
            pl.BlockSpec((MIX_ROWS, slots, pixel_count), lambda i: (i, 0, 0)),
            pl.BlockSpec((slots, entries), lambda i: (0, 0)),
        ],
        out_shape=[
            jax.ShapeDtypeStruct((row_count, slots, pixel_count), bf16),
            jax.ShapeDtypeStruct((slots, entries), f32),
        ],
        scratch_shapes=[pltpu.VMEM((2, entries * MIX_ROWS, pixel_count // 2), f32)],
        compiler_params=pltpu.CompilerParams(vmem_limit_bytes=VMEM_LIMIT),
        cost_estimate=pl.CostEstimate(
            flops=4 * row_count * slots * pixel_count * entries,
            bytes_accessed=2 * row_count * pixel_count * (2 * slots + entries),
            transcendentals=0,
        ),
        name="pixel_back",
    )(hyper, pixel_rows, *parts)


PAIR = [(0, 1), (1, 0)]
CORNER = [(i, i ^ 3) for i in range(4)]


def swap_core(value):
    return lax.ppermute(value, "c", PAIR)


def swap_x(value):
    return lax.ppermute(value, "x", PAIR)


def swap_plane(values):
    return [
        values[0],
        lax.ppermute(values[1], "y", PAIR),
        lax.ppermute(values[2], "x", PAIR),
        lax.ppermute(values[3], ("x", "y"), CORNER),
    ]


def body(
    pixels,
    wave_table,
    wave_weight,
    wave_bias,
    gen_weight,
    patch_bias,
    norm1_gain,
    norm1_bias,
    qkv_weight,
    query_bias,
    value_bias,
    out_weight,
    out_bias,
    norm2_gain,
    norm2_bias,
    fc1_weight,
    fc1_bias,
    fc2_weight,
    fc2_bias,
    band_count,
    band_table,
    cotangent,
):
    tile_count, seq_len, band_slots, pixel_count = pixels.shape[1:]
    model_width = gen_weight.shape[1]
    wave_width = wave_weight.shape[0]
    hidden_width = fc1_weight.shape[1]
    head_size = model_width // HEADS
    score_scale = head_size ** (-0.5)
    row_count = tile_count * seq_len
    head_shape = (tile_count, seq_len, HEADS, head_size)
    z_size = lax.axis_size("z")
    row_size = 2 * z_size
    at_x, at_c, at_y = lax.axis_index("x"), lax.axis_index("c"), lax.axis_index("y")
    quarter = 2 * at_x + at_c
    shard = qkv_weight.shape[0]
    unit = hidden_width // row_size // 4

    gen_rows = gen_weight.shape[0] // 4
    own_rows = lax.dynamic_slice_in_dim(gen_weight, quarter * gen_rows, gen_rows, 0)

    attn_pieces = jnp.stack(
        [qkv_weight[:, j * model_width : (j + 1) * model_width] for j in range(3)] + [out_weight]
    )
    fc1_pieces = fc1_weight.reshape(shard, row_size, 4, unit).transpose(2, 0, 1, 3)
    fc1_pieces = fc1_pieces.reshape(4, shard, row_size * unit)
    fc2_pieces = fc2_weight.reshape(4, unit, model_width)
    own_pieces = jnp.stack(
        [
            lax.dynamic_index_in_dim(pieces, quarter, 0, keepdims=False)
            for pieces in (attn_pieces, fc1_pieces, fc2_pieces)
        ]
    )
    gathered = lax.all_gather(own_pieces, ("z", "y"), axis=0, tiled=False)
    gathered = gathered.transpose(1, 0, 2, 3).reshape(3, model_width, model_width)
    other_core = swap_core(gathered)
    blocks = [gathered, other_core, swap_x(gathered), swap_x(other_core)]
    attn_blocks = jnp.stack([block[0] for block in blocks])
    w_query, w_key, w_value, w_out = (
        lax.dynamic_index_in_dim(attn_blocks, j ^ quarter, 0, keepdims=False) for j in range(4)
    )
    w_qkv = jnp.concatenate([w_query, w_key, w_value], axis=1)
    w_fc1 = jnp.concatenate([block[1] for block in blocks], axis=1)
    w_fc2 = jnp.concatenate([block[2] for block in blocks], axis=0)
    near = lax.all_gather(own_rows, "z", axis=0, tiled=True)
    far = swap_core(near)
    near = near.reshape(-1, pixel_count, model_width)
    far = far.reshape(-1, pixel_count, model_width)

    unit_order = fc1_bias.reshape(row_size, 4, unit).transpose(1, 0, 2).reshape(4, row_size * unit)
    bias_fc1 = jnp.concatenate(
        [lax.dynamic_index_in_dim(unit_order, quarter ^ d, 0, keepdims=False) for d in range(4)]
    )

    onehot = (band_table[0][:, None] == jnp.arange(wave_table.shape[0])[None, :]).astype(f32)
    wavelength = jnp.dot(onehot, wave_table, precision=highest)
    wave_embed = sincos(wavelength * 1000.0, wave_width)
    live = (jnp.arange(band_slots) < band_count[0]).astype(f32)[:, None]

    def hyper_fn(weight, bias):
        return jax.nn.gelu(jnp.dot(wave_embed, weight, precision=highest) + bias) * live

    hyper, hyper_back = jax.vjp(hyper_fn, wave_weight.astype(f32), wave_bias)
    per_row = wave_width // row_size
    place = jnp.arange(wave_width)
    kk = place % (per_row // 4)
    place = place // (per_row // 4)
    entry_z = place % z_size
    place = place // z_size
    entry_c, entry_y, entry_x = (place % 2) ^ at_c, (place // 2 % 2) ^ at_y, (place // 4) ^ at_x
    entry = per_row * (2 * entry_z + entry_y) + per_row // 4 * (2 * entry_x + entry_c) + kk
    order = (jnp.arange(wave_width)[:, None] == entry[None, :]).astype(bf16)
    hyper_low = dense_dot(hyper.astype(bf16), order).astype(bf16)

    pixel_rows = pixels.reshape(row_count, band_slots, pixel_count)
    patches = swap_plane(mix_pixels(hyper_low.T, pixel_rows))
    partial = project(patches, near, far)
    partial = swap_plane([partial[j * row_count : (j + 1) * row_count] for j in range(4)])
    projected = (partial[0] + partial[1]) + (partial[2] + partial[3])
    position = sincos(jnp.arange(seq_len).astype(f32), model_width)
    embedded = (projected + patch_bias).reshape(tile_count, seq_len, model_width) + position
    embedded = embedded.reshape(row_count, model_width)

    normed = layer_norm(embedded, norm1_gain, norm1_bias).astype(bf16)
    mixed = dense_dot(normed, w_qkv)
    queries = (mixed[:, :model_width] + query_bias).astype(bf16).reshape(head_shape)
    key_rows = mixed[:, model_width : 2 * model_width].astype(bf16).reshape(head_shape)
    value_rows = (mixed[:, 2 * model_width :] + value_bias).astype(bf16).reshape(head_shape)
    scores = (
        jnp.einsum("tqhd,tkhd->thqk", queries, key_rows, preferred_element_type=f32) * score_scale
    )
    probs_full = jax.nn.softmax(scores, axis=-1)
    probs = probs_full.astype(bf16)
    attended = (
        jnp.einsum("thqk,tkhd->tqhd", probs, value_rows, preferred_element_type=f32)
        .astype(bf16)
        .reshape(row_count, model_width)
    )
    middle = embedded + dense_dot(attended, w_out) + out_bias
    normed_two = layer_norm(middle, norm2_gain, norm2_bias).astype(bf16)
    fc_pre = dense_dot(normed_two, w_fc1) + bias_fc1
    hidden, gelu_back = jax.vjp(jax.nn.gelu, fc_pre)
    hidden = hidden.astype(bf16)
    block_out = middle + dense_dot(hidden, w_fc2) + fc2_bias

    grad_out = cotangent.reshape(row_count, model_width)
    fc2_bias_part = row_total(grad_out)
    fc2_grad = left_dot(hidden, grad_out)
    grad_hidden = right_dot(grad_out, w_fc2)
    grad_pre = gelu_back(grad_hidden)[0].astype(bf16)
    fc1_bias_part = row_total(grad_pre).reshape(4, row_size * unit)
    fc1_bias_part = jnp.stack(
        [lax.dynamic_index_in_dim(fc1_bias_part, quarter ^ j, 0, keepdims=False) for j in range(4)]
    )
    fc1_bias_part = fc1_bias_part.reshape(4, row_size, unit).transpose(1, 0, 2).reshape(-1)
    fc1_grad = left_dot(normed_two, grad_pre)
    grad_normed_two = right_dot(grad_pre, w_fc1)
    norm_two_back = jax.vjp(layer_norm, middle, norm2_gain, norm2_bias)[1]
    grad_middle, norm2_gain_part, norm2_bias_part = norm_two_back(grad_normed_two)
    grad_middle = grad_middle + grad_out.astype(f32)
    grad_branch = grad_middle.astype(bf16)
    out_bias_part = row_total(grad_branch)
    out_grad = left_dot(attended, grad_branch)
    grad_attended = right_dot(grad_branch, w_out).astype(bf16).reshape(head_shape)
    grad_probs = jnp.einsum(
        "tqhd,tkhd->thqk", grad_attended, value_rows, preferred_element_type=f32
    )
    grad_scores = probs_full * (
        grad_probs - jnp.sum(probs_full * grad_probs, axis=-1, keepdims=True)
    )
    grad_scores = grad_scores.astype(bf16)
    grad_queries = (
        jnp.einsum("thqk,tkhd->tqhd", grad_scores, key_rows, preferred_element_type=f32)
        * score_scale
    ).astype(bf16)
    grad_keys = (
        jnp.einsum("thqk,tqhd->tkhd", grad_scores, queries, preferred_element_type=f32)
        * score_scale
    ).astype(bf16)
    grad_values = jnp.einsum(
        "thqk,tqhd->tkhd", probs, grad_attended, preferred_element_type=f32
    ).astype(bf16)
    grad_queries = grad_queries.reshape(row_count, model_width)
    grad_values = grad_values.reshape(row_count, model_width)
    grad_mixed = jnp.concatenate(
        [grad_queries, grad_keys.reshape(row_count, model_width), grad_values], axis=1
    )
    query_bias_part = row_total(grad_queries)
    value_bias_part = row_total(grad_values)
    qkv_grad = left_dot(normed, grad_mixed)
    grad_normed = right_dot(grad_mixed, w_qkv)
    norm_one_back = jax.vjp(layer_norm, embedded, norm1_gain, norm1_bias)[1]
    grad_from_norm, norm1_gain_part, norm1_bias_part = norm_one_back(grad_normed)
    grad_embedded = (grad_middle + grad_from_norm).astype(bf16)
    patch_bias_part = row_total(grad_embedded)

    grads = jnp.concatenate(swap_plane([grad_embedded] * 4), axis=0)
    far_grad = swap_core(gen_grad(patches, grads, 1))
    back = swap_plane(back_patches(grads, near, far))
    near_grad = gen_grad(patches, grads, 0)
    gen_half = (near_grad.astype(f32) + far_grad.astype(f32)).astype(bf16)
    gen_half = gen_half.reshape(-1, model_width)
    gen_part = lax.psum_scatter(gen_half, "z", scatter_dimension=0, tiled=True)
    gen_total = lax.all_gather(gen_part, ("x", "c"), axis=0, tiled=True).astype(f32)

    attn_grads = jnp.stack(
        [qkv_grad[:, j * model_width : (j + 1) * model_width].astype(bf16) for j in range(3)]
        + [out_grad.astype(bf16)]
    )
    block_grads = []
    for d in range(4):
        cut = slice(d * model_width, (d + 1) * model_width)
        block_grads.append(
            jnp.stack(
                [
                    lax.dynamic_index_in_dim(attn_grads, quarter ^ d, 0, keepdims=False),
                    fc1_grad[:, cut].astype(bf16),
                    fc2_grad[cut].astype(bf16),
                ]
            )
        )
    received = swap_core(jnp.stack([block_grads[1], block_grads[3]]))
    kept = jnp.stack([block_grads[0], block_grads[2]])
    halves_sum = (kept.astype(f32) + received.astype(f32)).astype(bf16)
    received = swap_x(halves_sum[1])
    quarter_sum = (halves_sum[0].astype(f32) + received.astype(f32)).astype(bf16)
    pieces = lax.psum_scatter(quarter_sum, ("z", "y"), scatter_dimension=1, tiled=True)
    pieces = lax.all_gather(pieces, ("x", "c"), axis=0, tiled=False).astype(f32)
    qkv_total = jnp.concatenate([pieces[0, 0], pieces[1, 0], pieces[2, 0]], axis=1)
    out_total = pieces[3, 0]
    fc1_total = pieces[:, 1].reshape(4, shard, row_size, unit).transpose(1, 2, 0, 3)
    fc1_total = fc1_total.reshape(shard, hidden_width)
    fc2_total = pieces[:, 2].reshape(4 * unit, model_width)

    pixel_grad, grad_hyper = pixel_back(hyper_low, pixel_rows, back)
    grad_hyper = lax.dot_general(
        grad_hyper, order.astype(f32), (((1,), (1,)), ((), ())), precision=highest
    )
    wave_weight_part, wave_bias_part = hyper_back(grad_hyper)
    axes = ("x", "c", "z", "y")
    early = (
        patch_bias_part,
        norm1_gain_part,
        norm1_bias_part,
        query_bias_part,
        value_bias_part,
        out_bias_part,
        norm2_gain_part,
        norm2_bias_part,
        fc2_bias_part,
        fc1_bias_part,
    )
    early_total = lax.psum(jnp.concatenate(early), axes)
    early_total = [early_total[j * model_width : (j + 1) * model_width] for j in range(9)] + [
        early_total[9 * model_width :]
    ]
    (
        patch_bias_total,
        norm1_gain_total,
        norm1_bias_total,
        query_bias_total,
        value_bias_total,
        out_bias_total,
        norm2_gain_total,
        norm2_bias_total,
        fc2_bias_total,
        fc1_bias_total,
    ) = early_total
    late_total = lax.psum(jnp.concatenate([wave_weight_part, wave_bias_part[None]], axis=0), axes)
    wave_weight_total, wave_bias_total = late_total[:wave_width], late_total[wave_width]
    block_result = block_out.astype(bf16).reshape(1, tile_count, seq_len, model_width)
    pixel_result = pixel_grad.reshape(1, tile_count, seq_len, band_slots, pixel_count)
    return (
        block_result,
        pixel_result,
        wave_weight_total,
        wave_bias_total,
        gen_total,
        patch_bias_total,
        norm1_gain_total,
        norm1_bias_total,
        qkv_total,
        query_bias_total,
        value_bias_total,
        out_total,
        out_bias_total,
        norm2_gain_total,
        norm2_bias_total,
        fc1_total,
        fc1_bias_total,
        fc2_total,
        fc2_bias_total,
    )


def solution(mesh):
    grp_size, row_size = mesh.devices.shape
    split = Mesh(mesh.devices.reshape(grp_size // 2, 2, row_size // 2, 2), AXES)
    grp, row = ("x", "c"), ("z", "y")
    return jax.shard_map(
        body,
        mesh=split,
        in_specs=(
            P(grp, row, None, None, None),
            P(),
            P(),
            P(),
            P(row, None),
            P(),
            P(),
            P(),
            P(row, None),
            P(),
            P(),
            P(row, None),
            P(),
            P(),
            P(),
            P(row, None),
            P(),
            P(row, None),
            P(),
            P(grp),
            P(grp, None),
            P(grp, row, None, None),
        ),
        out_specs=(
            P(grp, row, None, None),
            P(grp, row, None, None, None),
            P(),
            P(),
            P(row, None),
            P(),
            P(),
            P(),
            P(row, None),
            P(),
            P(),
            P(row, None),
            P(),
            P(),
            P(),
            P(row, None),
            P(),
            P(row, None),
            P(),
        ),
        check_vma=False,
    )
```

```python
import functools

import jax
import jax.numpy as jnp
from jax import lax
from jax.experimental import pallas as pl
from jax.experimental.pallas import tpu as pltpu
from jax.sharding import Mesh
from jax.sharding import PartitionSpec as P

HEADS = 12

bf16 = jnp.bfloat16
f32 = jnp.float32
highest = lax.Precision.HIGHEST
epsilon = 1e-06

AXES = ("x", "c", "z", "y")
VMEM_LIMIT = 48 * 1024 * 1024
MIX_ROWS = 16
GEN_STEP = 4
COST = pl.CostEstimate(flops=1, bytes_accessed=1, transcendentals=0)


def sincos(angles_in, out_width):
    half_width = out_width // 2
    freqs = 1.0 / 10000.0 ** (jnp.arange(half_width).astype(angles_in.dtype) * (2.0 / out_width))
    angles = angles_in[:, None] * freqs[None, :]
    return jnp.concatenate([jnp.sin(angles), jnp.cos(angles)], axis=1)


def layer_norm(inputs, gain, shift):
    center = inputs - jnp.mean(inputs, axis=-1, keepdims=True)
    spread = jnp.mean(center * center, axis=-1, keepdims=True)
    return center * lax.rsqrt(spread + epsilon) * gain + shift


def dense_dot(left, right):
    return jnp.dot(left, right, preferred_element_type=f32)


def left_dot(left, right):
    return lax.dot_general(left, right, (((0,), (0,)), ((), ())), preferred_element_type=f32)


def right_dot(left, right):
    return lax.dot_general(left, right, (((1,), (1,)), ((), ())), preferred_element_type=f32)


def row_total(values):
    return jnp.sum(values.astype(f32), axis=0)


def mix_kernel(hyper_ref, pix_ref, *outs):
    slots, rows, pixel_count = pix_ref.shape
    entries = hyper_ref.shape[0]
    mixed = dense_dot(hyper_ref[...], pix_ref[...].reshape(slots, rows * pixel_count))
    mixed = mixed.astype(bf16).reshape(entries, rows, pixel_count)
    for j, out in enumerate(outs):
        share = out.shape[0]
        out[...] = mixed[j * share : (j + 1) * share]


def mix_pixels(hyper_t, pixel_rows):
    entries = hyper_t.shape[0]
    slots, row_count, pixel_count = pixel_rows.shape
    share = entries // 4
    out = jax.ShapeDtypeStruct((share, row_count, pixel_count), bf16)
    return pl.pallas_call(
        mix_kernel,
        grid=(row_count // MIX_ROWS,),
        in_specs=[
            pl.BlockSpec((entries, slots), lambda i: (0, 0)),
            pl.BlockSpec((slots, MIX_ROWS, pixel_count), lambda i: (0, i, 0)),
        ],
        out_specs=[pl.BlockSpec((share, MIX_ROWS, pixel_count), lambda i: (0, i, 0))] * 4,
        out_shape=[out] * 4,
        compiler_params=pltpu.CompilerParams(vmem_limit_bytes=VMEM_LIMIT),
        cost_estimate=COST,
        name="mix_pixels",
    )(hyper_t, pixel_rows)


def halves(steps):
    first = lambda i: (jnp.minimum(i, steps - 1), 0, 0)
    second = lambda i: (jnp.maximum(i - steps, 0), 0, 0)
    return first, second


def project_kernel(*refs):
    parts, w, sums, out = refs[:4], refs[4], refs[5:-1], refs[-1]

    @pl.when(pl.program_id(0) == 0)
    def _():
        out[...] = sums[0][...] if sums else jnp.zeros_like(out)

    for k in range(w.shape[0]):
        left = jnp.concatenate([a[k] for a in parts], axis=0)
        out[...] += dense_dot(left, w[k])


def project(parts, gen, which, sums=()):
    share, rows, pixel_count = parts[0].shape
    width = gen.shape[2]
    steps = share // 2 // GEN_STEP
    out = pl.BlockSpec((4 * rows, width), lambda i: (0, 0))
    return pl.pallas_call(
        project_kernel,
        grid=(steps,),
        in_specs=[pl.BlockSpec((GEN_STEP, rows, pixel_count), lambda i: (i + which * steps, 0, 0))] * 4
        + [pl.BlockSpec((GEN_STEP, pixel_count, width), lambda i: (i, 0, 0))]
        + [out] * len(sums),
        out_specs=out,
        out_shape=jax.ShapeDtypeStruct((4 * rows, width), f32),
        compiler_params=pltpu.CompilerParams(vmem_limit_bytes=VMEM_LIMIT),
        cost_estimate=COST,
        name="project",
    )(*parts, gen, *sums)


def early_rows(rows):
    return rows // 4 * 3


def back_kernel(g0, g1, g2, g3, w0, w1, *outs):
    i = pl.program_id(0)
    steps = pl.num_programs(0) // 2
    rows = g0.shape[0]

    def work(w):
        grads = jnp.concatenate([g[...] for g in (g0, g1, g2, g3)], axis=0)
        for k in range(w.shape[0]):
            res = right_dot(grads, w[k]).astype(bf16)
            for j, out in enumerate(outs):
                out[k] = res[j * rows : (j + 1) * rows]

    @pl.when(i < steps)
    def _():
        work(w0)

    @pl.when(i >= steps)
    def _():
        work(w1)


def back_patches(grads, near, far, start, rows):
    share, pixel_count, width = 2 * near.shape[0], near.shape[1], near.shape[2]
    steps = share // 2 // GEN_STEP
    first, second = halves(steps)
    out = jax.ShapeDtypeStruct((share, rows, pixel_count), bf16)
    return pl.pallas_call(
        back_kernel,
        grid=(2 * steps,),
        in_specs=[pl.BlockSpec((rows, width), lambda i: (start // rows, 0))] * 4
        + [
            pl.BlockSpec((GEN_STEP, pixel_count, width), first),
            pl.BlockSpec((GEN_STEP, pixel_count, width), second),
        ],
        out_specs=[pl.BlockSpec((GEN_STEP, rows, pixel_count), lambda i: (i, 0, 0))] * 4,
        out_shape=[out] * 4,
        compiler_params=pltpu.CompilerParams(vmem_limit_bytes=VMEM_LIMIT),
        cost_estimate=COST,
        name="back_patches",
    )(*grads, near, far)


def gen_grad_kernel(*refs, others):
    parts, grad_refs = refs[:4], refs[4:8]
    grads = jnp.concatenate([g[...] for g in grad_refs], axis=0)
    outs = refs[8 + others :]
    cut = outs[0].shape[1]
    for k in range(cut * len(outs)):
        left = jnp.concatenate([a[k] for a in parts], axis=0)
        res = left_dot(left, grads)
        for other in refs[8 : 8 + others]:
            res = res + other[k].astype(f32)
        outs[k // cut][0, k % cut] = res.astype(bf16)


def gen_grad(parts, grads, which, others=(), chunks=1):
    share, rows, pixel_count = parts[0].shape
    width = grads[0].shape[1]
    steps = share // 2 // GEN_STEP
    cut = GEN_STEP // chunks
    return pl.pallas_call(
        functools.partial(gen_grad_kernel, others=len(others)),
        grid=(steps,),
        in_specs=[pl.BlockSpec((GEN_STEP, rows, pixel_count), lambda i: (i + which * steps, 0, 0))] * 4
        + [pl.BlockSpec((rows, width), lambda i: (0, 0))] * 4
        + [pl.BlockSpec((GEN_STEP, pixel_count, width), lambda i: (i, 0, 0))] * len(others),
        out_specs=[pl.BlockSpec((1, cut, pixel_count, width), lambda i: (i, 0, 0, 0))] * chunks,
        out_shape=[jax.ShapeDtypeStruct((steps, cut, pixel_count, width), bf16)] * chunks,
        compiler_params=pltpu.CompilerParams(vmem_limit_bytes=VMEM_LIMIT),
        cost_estimate=COST,
        name="gen_grad",
    )(*parts, *grads, *others)


def pixel_kernel(hyper_ref, pix_ref, g0, g1, g2, g3, *refs):
    grad_ref, total_ref = refs[-2:]
    slots, rows, pixel_count = pix_ref.shape
    entries = hyper_ref.shape[1]

    @pl.when(pl.program_id(0) == 0)
    def _():
        total_ref[...] = jnp.zeros_like(total_ref)

    grad = jnp.concatenate([g[...] for g in (g0, g1, g2, g3)], axis=0)
    grad = grad.reshape(entries, rows * pixel_count)
    pix = pix_ref[...].reshape(slots, rows * pixel_count)
    out = dense_dot(hyper_ref[...], grad).astype(bf16)
    grad_ref[...] = out.reshape(slots, rows, pixel_count)
    total_ref[...] += right_dot(pix, grad)


def pixel_back(hyper, pixel_rows, parts, start, before=()):
    slots, entries = hyper.shape
    _, row_count, pixel_count = pixel_rows.shape
    share, rows, _ = parts[0].shape
    block = pl.BlockSpec((slots, MIX_ROWS, pixel_count), lambda i: (0, start // MIX_ROWS + i, 0))
    return pl.pallas_call(
        pixel_kernel,
        grid=(rows // MIX_ROWS,),
        in_specs=[pl.BlockSpec((slots, entries), lambda i: (0, 0)), block]
        + [pl.BlockSpec((share, MIX_ROWS, pixel_count), lambda i: (0, i, 0))] * 4
        + [pl.BlockSpec(memory_space=pl.ANY)] * len(before),
        out_specs=[block, pl.BlockSpec((slots, entries), lambda i: (0, 0))],
        out_shape=[
            jax.ShapeDtypeStruct((slots, row_count, pixel_count), bf16),
            jax.ShapeDtypeStruct((slots, entries), f32),
        ],
        input_output_aliases={6: 0} if before else {},
        compiler_params=pltpu.CompilerParams(vmem_limit_bytes=VMEM_LIMIT),
        cost_estimate=COST,
        name="pixel_back",
    )(hyper, pixel_rows, *parts, *before)


def put_kernel(at_ref, *refs, count):
    for j in range(count):

        @pl.when(pl.program_id(0) == j)
        def _(j=j):
            refs[-1][...] = refs[j][...].astype(f32)


def put_parts(pieces, quarters, chunk, chunks, before=()):
    rows, width = pieces[0].shape
    count = len(pieces)
    return pl.pallas_call(
        functools.partial(put_kernel, count=count),
        grid_spec=pltpu.PrefetchScalarGridSpec(
            num_scalar_prefetch=1,
            grid=(count,),
            in_specs=[pl.BlockSpec((rows, width), lambda i, at_ref: (0, 0))] * count
            + [pl.BlockSpec(memory_space=pl.ANY)] * len(before),
            out_specs=pl.BlockSpec((rows, width), lambda i, at_ref: (at_ref[i] * chunks + chunk, 0)),
        ),
        out_shape=jax.ShapeDtypeStruct((4 * chunks * rows, width), f32),
        input_output_aliases={1 + count: 0} if before else {},
        compiler_params=pltpu.CompilerParams(vmem_limit_bytes=VMEM_LIMIT),
        cost_estimate=COST,
        name="put_parts",
    )(jnp.stack(quarters), *pieces, *before)


PAIR = [(0, 1), (1, 0)]
CORNER = [(i, i ^ 3) for i in range(4)]


def swap_core(value):
    return lax.ppermute(value, "c", PAIR)


def swap_x(value):
    return lax.ppermute(value, "x", PAIR)


def swap_y(value):
    return lax.ppermute(value, "y", PAIR)


def swap_plane(values):
    return [
        values[0],
        swap_y(values[1]),
        swap_x(values[2]),
        lax.ppermute(values[3], ("x", "y"), CORNER),
    ]


def after(values, *earlier):
    return lax.optimization_barrier((values, earlier))[0]


def pick(pieces, index):
    return lax.dynamic_index_in_dim(pieces, index, 0, keepdims=False)


UP, DOWN = ([(i, (i + step) % 4) for i in range(4)] for step in (1, 3))


def gather_z(own):
    size, at = lax.axis_size("z"), lax.axis_index("z")
    if size != 4:
        return lax.all_gather(own, "z", axis=0, tiled=False)
    half = own.shape[-2] // 2
    below, above = lax.ppermute(own, "z", UP), lax.ppermute(own, "z", DOWN)
    across = [
        lax.ppermute(below[..., :half, :], "z", UP),
        lax.ppermute(above[..., half:, :], "z", DOWN),
    ]
    out = jnp.zeros((4,) + own.shape, own.dtype)
    for piece, step in ((own, 0), (below, 3), (above, 1), (jnp.concatenate(across, axis=-2), 2)):
        out = lax.dynamic_update_index_in_dim(out, piece, (at + step) % 4, 0)
    return out


def scatter_z(pieces):
    size, at = lax.axis_size("z"), lax.axis_index("z")
    if size != 4:
        return lax.psum_scatter(pieces, "z", scatter_dimension=0, tiled=False)
    half = pieces.shape[-2] // 2
    own, above, across, below = (pick(pieces, (at + step) % 4) for step in range(4))
    from_below = lax.ppermute(across[..., :half, :], "z", UP)
    from_above = lax.ppermute(across[..., half:, :], "z", DOWN)
    above = jnp.concatenate([add_low(above[..., :half, :], from_below), above[..., half:, :]], axis=-2)
    below = jnp.concatenate([below[..., :half, :], add_low(below[..., half:, :], from_above)], axis=-2)
    total = own.astype(f32) + lax.ppermute(above, "z", UP).astype(f32)
    return (total + lax.ppermute(below, "z", DOWN).astype(f32)).astype(bf16)


def gather_quarters(own, quarter):
    across = swap_x(own)
    away = jnp.stack([own, swap_core(own), across, swap_core(across)])
    return jnp.stack([pick(away, quarter ^ j) for j in range(4)])


def total_of(value, earlier):
    value = value + swap_core(value)
    value = value + swap_x(value)
    value = after(value, earlier)
    value = value + swap_y(value)
    size, step = lax.axis_size("z"), 1
    while step < size:
        value = value + lax.ppermute(value, "z", [(i, i ^ step) for i in range(size)])
        step *= 2
    return value


def reduce_core(blocks):
    return [split_y(add_low(blocks[2 * dx], swap_core(blocks[2 * dx + 1]))) for dx in range(2)]


def add_low(left, right):
    return (left.astype(f32) + right.astype(f32)).astype(bf16)


def split_y(block):
    size = lax.axis_size("z")
    return block.reshape(size, 2, block.shape[0] // size // 2, block.shape[1])


def of_y(block, y):
    return lax.dynamic_index_in_dim(block, y, 1, keepdims=False)


def join_y(own, other):
    at_y = lax.axis_index("y")
    both = [jnp.where(at_y == 0, own, other), jnp.where(at_y == 0, other, own)]
    return jnp.stack(both, axis=1).reshape(-1, own.shape[-1])


def gather_start(column):
    half = column.shape[0] // 2
    return swap_y(column[:half]), swap_x(column[half:])


def gather_more(column, came):
    half, kinds = column.shape[0] // 2, column.shape[1]
    low = jnp.stack([join_y(column[:half, kind], came[0][:, kind]) for kind in range(kinds)])
    high = jnp.stack([column[half:], came[1]])
    return low, high


def gather_end(low, high, low_x, high_y):
    return [
        [
            jnp.concatenate([from_low[kind], join_y(high[dx][:, kind], high_y[dx][:, kind])])
            for dx, from_low in enumerate((low, low_x))
        ]
        for kind in range(low.shape[0])
    ]


def sum_start(blocks):
    at_y, half = lax.axis_index("y"), blocks[0][0].shape[0] // 2
    to_y = jnp.stack([jnp.stack([of_y(b[:half], 1 - at_y) for b in pair]) for pair in blocks])
    return to_y, jnp.stack([pair[1][half:] for pair in blocks])


def sum_more(blocks, from_y, from_x):
    at_y, half = lax.axis_index("y"), blocks[0][0].shape[0] // 2
    low = [
        jnp.stack([add_low(of_y(pair[dx][:half], at_y), from_y[kind, dx]) for kind, pair in enumerate(blocks)])
        for dx in range(2)
    ]
    high = [
        jnp.stack([add_low(of_y(pair[0][half:], y), of_y(from_x[kind], y)) for kind, pair in enumerate(blocks)])
        for y in (at_y, 1 - at_y)
    ]
    return low[0], high[0], low[1], high[1]


def sum_end(low, high, low_x, high_y):
    return jnp.concatenate([add_low(low, low_x), add_low(high, high_y)], axis=1).swapaxes(0, 1)


def body(
    pixels,
    wave_table,
    wave_weight,
    wave_bias,
    gen_weight,
    patch_bias,
    norm1_gain,
    norm1_bias,
    qkv_weight,
    query_bias,
    value_bias,
    out_weight,
    out_bias,
    norm2_gain,
    norm2_bias,
    fc1_weight,
    fc1_bias,
    fc2_weight,
    fc2_bias,
    band_count,
    band_table,
    cotangent,
):
    tile_count, seq_len, band_slots, pixel_count = pixels.shape[1:]
    model_width = gen_weight.shape[1]
    wave_width = wave_weight.shape[0]
    hidden_width = fc1_weight.shape[1]
    head_size = model_width // HEADS
    score_scale = head_size ** (-0.5)
    row_count = tile_count * seq_len
    head_shape = (tile_count, seq_len, HEADS, head_size)
    z_size = lax.axis_size("z")
    row_size = 2 * z_size
    at_x, at_c, at_y = lax.axis_index("x"), lax.axis_index("c"), lax.axis_index("y")
    quarter = 2 * at_x + at_c
    shard = qkv_weight.shape[0]
    unit = hidden_width // row_size // 4

    gen_rows = gen_weight.shape[0] // 4
    own_rows = lax.dynamic_slice_in_dim(gen_weight, quarter * gen_rows, gen_rows, 0)
    near = lax.all_gather(own_rows, "z", axis=0, tiled=True)

    unit_order = fc1_bias.reshape(row_size, 4, unit).transpose(1, 0, 2).reshape(4, row_size * unit)
    bias_fc1 = [pick(unit_order, quarter ^ d) for d in range(4)]

    onehot = (band_table[0][:, None] == jnp.arange(wave_table.shape[0])[None, :]).astype(f32)
    wavelength = jnp.dot(onehot, wave_table, precision=highest)
    wave_embed = sincos(wavelength * 1000.0, wave_width)
    live = (jnp.arange(band_slots) < band_count[0]).astype(f32)[:, None]

    def hyper_fn(weight, bias):
        return jax.nn.gelu(jnp.dot(wave_embed, weight, precision=highest) + bias) * live

    hyper, hyper_back = jax.vjp(hyper_fn, wave_weight.astype(f32), wave_bias)
    per_row = wave_width // row_size
    place = jnp.arange(wave_width)
    kk = place % (per_row // 4)
    place = place // (per_row // 4)
    entry_z = place % z_size
    place = place // z_size
    entry_c, entry_y, entry_x = (place % 2) ^ at_c, (place // 2 % 2) ^ at_y, (place // 4) ^ at_x
    entry = per_row * (2 * entry_z + entry_y) + per_row // 4 * (2 * entry_x + entry_c) + kk
    order = (jnp.arange(wave_width)[:, None] == entry[None, :]).astype(bf16)
    hyper_low = dense_dot(hyper.astype(bf16), order).astype(bf16)

    pixel_rows = pixels.reshape(row_count, band_slots, pixel_count).transpose(1, 0, 2)
    mixed_pixels = mix_pixels(hyper_low.T, pixel_rows)
    patches = swap_plane(mixed_pixels)

    weights = (qkv_weight, out_weight, fc1_weight, fc2_weight)
    qkv_weight, out_weight, fc1_weight, fc2_weight = after(weights, mixed_pixels)
    attn_piece = pick(
        jnp.stack(
            [qkv_weight[:, j * model_width : (j + 1) * model_width] for j in range(3)] + [out_weight]
        ),
        quarter,
    )
    fc1_piece = lax.dynamic_index_in_dim(fc1_weight.reshape(shard, row_size, 4, unit), quarter, 2, False)
    fc1_piece = fc1_piece.reshape(shard, row_size * unit)
    fc2_piece = pick(fc2_weight.reshape(4, unit, model_width), quarter)
    column = gather_z(jnp.stack([attn_piece, fc1_piece, fc2_piece]))
    low, high = gather_more(column, gather_start(column))
    low, high, patches = after((low, high, patches))
    near = after(near, low, high)
    far = swap_core(near)
    near = near.reshape(-1, pixel_count, model_width)
    far = far.reshape(-1, pixel_count, model_width)
    attn_came = swap_x(low[:1]), swap_y(high[:, :, :1])
    partial = project(patches, far, 1, (project(patches, near, 0),))
    partial = [partial[j * row_count : (j + 1) * row_count] for j in range(4)]
    partial = [partial[0]] + swap_plane([piece.astype(bf16) for piece in partial])[1:]
    projected = (partial[0] + partial[1]) + (partial[2] + partial[3])
    attn_came, fc_low, fc_high = after((attn_came, low[1:], high[:, :, 1:]), projected)
    fc_came = swap_x(fc_low), swap_y(fc_high)

    def both_cores(blocks):
        return [block for owned in blocks for block in (owned, swap_core(owned))]

    attn = jnp.stack(both_cores(gather_end(low[:1], high[:, :, :1], *attn_came)[0]))
    w_query, w_key, w_value, w_out = (pick(attn, j ^ quarter) for j in range(4))
    position = sincos(jnp.arange(seq_len).astype(f32), model_width)
    embedded = (projected + patch_bias).reshape(tile_count, seq_len, model_width) + position
    embedded = embedded.reshape(row_count, model_width)

    normed = layer_norm(embedded, norm1_gain, norm1_bias).astype(bf16)
    queries = (dense_dot(normed, w_query) + query_bias).astype(bf16).reshape(head_shape)
    key_rows = dense_dot(normed, w_key).astype(bf16).reshape(head_shape)
    value_rows = (dense_dot(normed, w_value) + value_bias).astype(bf16).reshape(head_shape)
    scores = (
        jnp.einsum("tqhd,tkhd->thqk", queries, key_rows, preferred_element_type=f32) * score_scale
    )
    probs_full = jax.nn.softmax(scores, axis=-1)
    probs = probs_full.astype(bf16)
    attended = (
        jnp.einsum("thqk,tkhd->tqhd", probs, value_rows, preferred_element_type=f32)
        .astype(bf16)
        .reshape(row_count, model_width)
    )
    middle = embedded + dense_dot(attended, w_out) + out_bias
    fc_came = after(fc_came, middle)
    w_fc1, w_fc2 = (both_cores(blocks) for blocks in gather_end(fc_low, fc_high, *fc_came))
    normed_two = layer_norm(middle, norm2_gain, norm2_bias).astype(bf16)
    fc_pre = [dense_dot(normed_two, w) + bias for w, bias in zip(w_fc1, bias_fc1)]
    hidden, gelu_back = zip(*(jax.vjp(jax.nn.gelu, values) for values in fc_pre))
    hidden = [values.astype(bf16) for values in hidden]
    block_out = middle + sum(dense_dot(values, w) for values, w in zip(hidden, w_fc2)) + fc2_bias

    grad_out = cotangent.reshape(row_count, model_width)
    fc2_bias_part = row_total(grad_out)
    grad_pre = [
        back(right_dot(grad_out, w))[0].astype(bf16) for back, w in zip(gelu_back, w_fc2)
    ]
    fc1_bias_part = jnp.stack([row_total(values) for values in grad_pre])
    fc1_bias_part = jnp.stack([pick(fc1_bias_part, quarter ^ j) for j in range(4)])
    fc1_bias_part = fc1_bias_part.reshape(4, row_size, unit).transpose(1, 0, 2).reshape(-1)
    grad_normed_two = sum(right_dot(values, w) for values, w in zip(grad_pre, w_fc1))
    norm_two_back = jax.vjp(layer_norm, middle, norm2_gain, norm2_bias)[1]
    grad_middle, norm2_gain_part, norm2_bias_part = norm_two_back(grad_normed_two)
    grad_middle = grad_middle + grad_out.astype(f32)
    grad_branch = grad_middle.astype(bf16)
    out_bias_part = row_total(grad_branch)
    grad_attended = right_dot(grad_branch, w_out).astype(bf16).reshape(head_shape)
    grad_probs = jnp.einsum(
        "tqhd,tkhd->thqk", grad_attended, value_rows, preferred_element_type=f32
    )
    grad_scores = probs_full * (
        grad_probs - jnp.sum(probs_full * grad_probs, axis=-1, keepdims=True)
    )
    grad_scores = grad_scores.astype(bf16)
    grad_queries = (
        jnp.einsum("thqk,tkhd->tqhd", grad_scores, key_rows, preferred_element_type=f32)
        * score_scale
    ).astype(bf16)
    grad_keys = (
        jnp.einsum("thqk,tqhd->tkhd", grad_scores, queries, preferred_element_type=f32)
        * score_scale
    ).astype(bf16)
    grad_values = jnp.einsum(
        "thqk,tqhd->tkhd", probs, grad_attended, preferred_element_type=f32
    ).astype(bf16)
    grad_queries = grad_queries.reshape(row_count, model_width)
    grad_values = grad_values.reshape(row_count, model_width)
    grad_keys = grad_keys.reshape(row_count, model_width)
    query_bias_part = row_total(grad_queries)
    value_bias_part = row_total(grad_values)
    grad_normed = right_dot(grad_queries, w_query)
    grad_normed += right_dot(grad_keys, w_key)
    grad_normed += right_dot(grad_values, w_value)
    norm_one_back = jax.vjp(layer_norm, embedded, norm1_gain, norm1_bias)[1]
    grad_from_norm, norm1_gain_part, norm1_bias_part = norm_one_back(grad_normed)
    grad_embedded = (grad_middle + grad_from_norm).astype(bf16)
    patch_bias_part = row_total(grad_embedded)

    grads = swap_plane([grad_embedded] * 4)
    (far_grad,) = gen_grad(patches, grads, 1)
    far_grad = swap_core(far_grad.reshape(-1, pixel_count, model_width))
    early = early_rows(row_count)
    back_early = back_patches(grads, near, far, 0, early)
    far_grad = after(far_grad, back_early)
    back_early = swap_plane(back_early)
    chunks = 2 if wave_width // row_size // 4 == GEN_STEP else 1
    gen_sent = gen_grad(patches, grads, 0, (far_grad,), chunks)
    gen_parts = [
        lax.psum_scatter(chunk.reshape(-1, model_width), "z", scatter_dimension=0, tiled=True)
        for chunk in gen_sent
    ]

    left = jnp.stack([normed, normed, normed, attended])
    right = jnp.stack([grad_queries, grad_keys, grad_values, grad_branch])
    near_first = [0, 2, 1, 3]
    left = jnp.stack([pick(left, quarter ^ d) for d in near_first])
    right = jnp.stack([pick(right, quarter ^ d) for d in near_first])
    hidden, grad_pre = (jnp.stack([values[d] for d in near_first]) for values in (hidden, grad_pre))
    sides = [(left, right), (jnp.stack([normed_two] * 2), grad_pre), (hidden, jnp.stack([grad_out] * 2))]
    sides = after(sides, gen_sent)

    def block_grad(side, part):
        return jnp.einsum(
            "dri,drj->dij", *(v if v.shape[0] == 2 else v[part : part + 2] for v in side), preferred_element_type=f32
        ).astype(bf16)

    block_grads = [swap_core(block_grad(side, 2)) for side in sides]
    block_grads = [add_low(block_grad(side, 0), came) for side, came in zip(sides, block_grads)]
    block_grads = [[split_y(pair[dx]) for dx in range(2)] for pair in block_grads]
    to_y, to_x = sum_start(block_grads)
    back_late = back_patches(after(grads, gen_sent), near, far, early, row_count - early)
    to_y, to_x, back_early, back_late = after((to_y, to_x, back_early, back_late))
    back_late = swap_plane(back_late)
    from_y, from_x = swap_y(to_y), swap_x(to_x)
    pixel_grad, hyper_early = pixel_back(hyper_low, pixel_rows, back_early, 0)
    back_late, from_y, from_x, hyper_early = after((back_late, from_y, from_x, hyper_early))
    low, high, low_sent, high_sent = sum_more(block_grads, from_y, from_x)
    low_x, high_y = swap_x(low_sent), swap_y(high_sent)
    across = [swap_x(gen_parts[0])]
    pixel_grad, hyper_late = pixel_back(hyper_low, pixel_rows, back_late, early, (pixel_grad,))
    low_x, high_y, hyper_late = after((low_x, high_y, hyper_late), across)
    across += [swap_x(piece) for piece in gen_parts[1:]]
    share_sum = scatter_z(sum_end(low, high, low_x, high_y))
    totals = gather_quarters(share_sum, quarter).astype(f32)
    qkv_total = jnp.concatenate([totals[0, 0], totals[1, 0], totals[2, 0]], axis=1)
    out_total = totals[3, 0]
    fc1_total = totals[:, 1].reshape(4, shard, row_size, unit).transpose(1, 2, 0, 3)
    fc1_total = fc1_total.reshape(shard, hidden_width)
    fc2_total = totals[:, 2].reshape(4 * unit, model_width)

    grad_hyper = hyper_early + hyper_late
    grad_hyper = lax.dot_general(
        grad_hyper, order.astype(f32), (((1,), (1,)), ((), ())), precision=highest
    )
    wave_weight_part, wave_bias_part = hyper_back(grad_hyper)
    small = (
        patch_bias_part,
        norm1_gain_part,
        norm1_bias_part,
        query_bias_part,
        value_bias_part,
        out_bias_part,
        norm2_gain_part,
        norm2_bias_part,
        fc2_bias_part,
        fc1_bias_part,
    )
    small = jnp.concatenate(small + (wave_bias_part,)).reshape(-1, wave_width)
    small = total_of(jnp.concatenate([wave_weight_part, small]), across)
    gen_total = ()
    for chunk, piece in enumerate(gen_parts):
        pair = piece, swap_core(piece)
        gen_total = (put_parts(pair, (quarter, quarter ^ 1), chunk, chunks, gen_total),)
        pair = across[chunk], swap_core(across[chunk])
        gen_total = (put_parts(pair, (quarter ^ 2, quarter ^ 3), chunk, chunks, gen_total),)
    gen_total = gen_total[0]
    wave_weight_total, small = small[:wave_width], small[wave_width:].reshape(-1)
    cuts = [model_width * j for j in range(1, 10)] + [9 * model_width + hidden_width]
    (
        patch_bias_total,
        norm1_gain_total,
        norm1_bias_total,
        query_bias_total,
        value_bias_total,
        out_bias_total,
        norm2_gain_total,
        norm2_bias_total,
        fc2_bias_total,
        fc1_bias_total,
        wave_bias_total,
    ) = jnp.split(small, cuts)
    block_result = block_out.astype(bf16).reshape(1, tile_count, seq_len, model_width)
    pixel_result = pixel_grad.transpose(1, 0, 2).reshape(1, tile_count, seq_len, band_slots, pixel_count)
    return (
        block_result,
        pixel_result,
        wave_weight_total,
        wave_bias_total,
        gen_total,
        patch_bias_total,
        norm1_gain_total,
        norm1_bias_total,
        qkv_total,
        query_bias_total,
        value_bias_total,
        out_total,
        out_bias_total,
        norm2_gain_total,
        norm2_bias_total,
        fc1_total,
        fc1_bias_total,
        fc2_total,
        fc2_bias_total,
    )


def solution(mesh):
    grp_size, row_size = mesh.devices.shape
    split = Mesh(mesh.devices.reshape(grp_size // 2, 2, row_size // 2, 2), AXES)
    grp, row = ("x", "c"), ("z", "y")
    return jax.shard_map(
        body,
        mesh=split,
        in_specs=(
            P(grp, row, None, None, None),
            P(),
            P(),
            P(),
            P(row, None),
            P(),
            P(),
            P(),
            P(row, None),
            P(),
            P(),
            P(row, None),
            P(),
            P(),
            P(),
            P(row, None),
            P(),
            P(row, None),
            P(),
            P(grp),
            P(grp, None),
            P(grp, row, None, None),
        ),
        out_specs=(
            P(grp, row, None, None),
            P(grp, row, None, None, None),
            P(),
            P(),
            P(row, None),
            P(),
            P(),
            P(),
            P(row, None),
            P(),
            P(),
            P(row, None),
            P(),
            P(),
            P(),
            P(row, None),
            P(),
            P(row, None),
            P(),
        ),
        check_vma=False,
    )
```

```python
import functools

import jax
import jax.numpy as jnp
import numpy as np
from jax import lax
from jax.experimental import pallas as pl
from jax.experimental.pallas import tpu as pltpu
from jax.sharding import Mesh
from jax.sharding import PartitionSpec as P

HEADS = 12

bf16 = jnp.bfloat16
f32 = jnp.float32
highest = lax.Precision.HIGHEST
epsilon = 1e-06

AXES = ("x", "c", "z", "y")
PLANNED = (4, 8)
VMEM_LIMIT = 48 * 1024 * 1024
MIX_ROWS = 16
GEN_STEP = 4
COST = pl.CostEstimate(flops=1, bytes_accessed=1, transcendentals=0)


def sincos(angles_in, out_width):
    half_width = out_width // 2
    freqs = 1.0 / 10000.0 ** (jnp.arange(half_width).astype(angles_in.dtype) * (2.0 / out_width))
    angles = angles_in[:, None] * freqs[None, :]
    return jnp.concatenate([jnp.sin(angles), jnp.cos(angles)], axis=1)


def layer_norm(inputs, gain, shift):
    center = inputs - jnp.mean(inputs, axis=-1, keepdims=True)
    spread = jnp.mean(center * center, axis=-1, keepdims=True)
    return center * lax.rsqrt(spread + epsilon) * gain + shift


def dense_dot(left, right):
    return jnp.dot(left, right, preferred_element_type=f32)


def left_dot(left, right):
    return lax.dot_general(left, right, (((0,), (0,)), ((), ())), preferred_element_type=f32)


def right_dot(left, right):
    return lax.dot_general(left, right, (((1,), (1,)), ((), ())), preferred_element_type=f32)


def row_total(values):
    return jnp.sum(values.astype(f32), axis=0, keepdims=True)


def mix_kernel(hyper_ref, pix_ref, *outs):
    slots, rows, pixel_count = pix_ref.shape
    entries = hyper_ref.shape[0]
    mixed = dense_dot(hyper_ref[...], pix_ref[...].reshape(slots, rows * pixel_count))
    mixed = mixed.astype(bf16).reshape(entries, rows, pixel_count)
    for j, out in enumerate(outs):
        share = out.shape[0]
        out[...] = mixed[j * share : (j + 1) * share]


def mix_pixels(hyper_t, pixel_rows):
    entries = hyper_t.shape[0]
    slots, row_count, pixel_count = pixel_rows.shape
    share = entries // 4
    out = jax.ShapeDtypeStruct((share, row_count, pixel_count), bf16)
    return pl.pallas_call(
        mix_kernel,
        grid=(row_count // MIX_ROWS,),
        in_specs=[
            pl.BlockSpec((entries, slots), lambda i: (0, 0)),
            pl.BlockSpec((slots, MIX_ROWS, pixel_count), lambda i: (0, i, 0)),
        ],
        out_specs=[pl.BlockSpec((share, MIX_ROWS, pixel_count), lambda i: (0, i, 0))] * 4,
        out_shape=[out] * 4,
        compiler_params=pltpu.CompilerParams(vmem_limit_bytes=VMEM_LIMIT),
        cost_estimate=COST,
        name="mix_pixels",
    )(hyper_t, pixel_rows)


def project_kernel(a0, a1, a2, a3, w, out):
    @pl.when(pl.program_id(0) == 0)
    def _():
        out[...] = jnp.zeros_like(out)

    for k in range(w.shape[0]):
        left = jnp.concatenate([a[k] for a in (a0, a1, a2, a3)], axis=0)
        out[...] += dense_dot(left, w[k])


def project(parts, gen):
    share, rows, pixel_count = parts[0].shape
    width = gen.shape[2]
    return pl.pallas_call(
        project_kernel,
        grid=(share // GEN_STEP,),
        in_specs=[pl.BlockSpec((GEN_STEP, rows, pixel_count), lambda i: (i, 0, 0))] * 4
        + [pl.BlockSpec((GEN_STEP, pixel_count, width), lambda i: (i, 0, 0))],
        out_specs=pl.BlockSpec((4 * rows, width), lambda i: (0, 0)),
        out_shape=jax.ShapeDtypeStruct((4 * rows, width), f32),
        compiler_params=pltpu.CompilerParams(vmem_limit_bytes=VMEM_LIMIT),
        cost_estimate=COST,
        name="project",
    )(*parts, gen)


def early_rows(rows):
    return rows // 4 * 3


def back_kernel(g0, g1, g2, g3, w, *outs):
    rows = g0.shape[0]
    grads = jnp.concatenate([g[...] for g in (g0, g1, g2, g3)], axis=0)
    for k in range(w.shape[0]):
        res = right_dot(grads, w[k]).astype(bf16)
        for j, out in enumerate(outs):
            out[k] = res[j * rows : (j + 1) * rows]


def back_patches(grads, gen, start, rows):
    share, pixel_count, width = gen.shape
    return pl.pallas_call(
        back_kernel,
        grid=(share // GEN_STEP,),
        in_specs=[pl.BlockSpec((rows, width), lambda i: (start // rows, 0))] * 4
        + [pl.BlockSpec((GEN_STEP, pixel_count, width), lambda i: (i, 0, 0))],
        out_specs=[pl.BlockSpec((GEN_STEP, rows, pixel_count), lambda i: (i, 0, 0))] * 4,
        out_shape=[jax.ShapeDtypeStruct((share, rows, pixel_count), bf16)] * 4,
        compiler_params=pltpu.CompilerParams(vmem_limit_bytes=VMEM_LIMIT),
        cost_estimate=COST,
        name="back_patches",
    )(*grads, gen)


def gen_grad_kernel(core_ref, *refs):
    parts, grad_refs, outs = refs[:8], refs[8:13], refs[13:]
    grads = jnp.concatenate([g[...] for g in grad_refs], axis=0)
    cut = outs[0].shape[1]
    for k in range(cut * len(outs)):
        left = jnp.concatenate([a[k] for a in parts], axis=0)
        outs[k // cut][0, k % cut] = left_dot(left, grads).astype(bf16)


def gen_grad(parts, others, grads, other_grads, chunks, at_c):
    share, rows, pixel_count = others[0].shape
    width = other_grads.shape[1]
    steps = share // 2 // GEN_STEP
    cut = GEN_STEP // chunks
    block = (GEN_STEP, rows, pixel_count)
    return pl.pallas_call(
        gen_grad_kernel,
        grid_spec=pltpu.PrefetchScalarGridSpec(
            num_scalar_prefetch=1,
            grid=(steps,),
            in_specs=[pl.BlockSpec(block, lambda i, core: (core[0] * steps + i, 0, 0))] * 8
            + [pl.BlockSpec((rows, width), lambda i, core: (0, 0))] * 4
            + [pl.BlockSpec((4 * rows, width), lambda i, core: (0, 0))],
            out_specs=[pl.BlockSpec((1, cut, pixel_count, width), lambda i, core: (i, 0, 0, 0))] * chunks,
        ),
        out_shape=[jax.ShapeDtypeStruct((steps, cut, pixel_count, width), bf16)] * chunks,
        compiler_params=pltpu.CompilerParams(vmem_limit_bytes=VMEM_LIMIT),
        cost_estimate=COST,
        name="gen_grad",
    )(at_c.reshape(1), *parts, *others, *grads, other_grads)


def pixel_kernel(hyper_ref, pix_ref, g0, g1, g2, g3, *refs):
    grad_ref, total_ref = refs[-2:]
    slots, rows, pixel_count = pix_ref.shape
    entries = hyper_ref.shape[1]

    @pl.when(pl.program_id(0) == 0)
    def _():
        total_ref[...] = jnp.zeros_like(total_ref)

    grad = jnp.concatenate([g[...] for g in (g0, g1, g2, g3)], axis=0)
    grad = grad.reshape(entries, rows * pixel_count)
    pix = pix_ref[...].reshape(slots, rows * pixel_count)
    out = dense_dot(hyper_ref[...], grad).astype(bf16)
    grad_ref[...] = out.reshape(slots, rows, pixel_count)
    total_ref[...] += right_dot(pix, grad)


def pixel_back(hyper, pixel_rows, parts, start, before=()):
    slots, entries = hyper.shape
    _, row_count, pixel_count = pixel_rows.shape
    share, rows, _ = parts[0].shape
    block = pl.BlockSpec((slots, MIX_ROWS, pixel_count), lambda i: (0, start // MIX_ROWS + i, 0))
    return pl.pallas_call(
        pixel_kernel,
        grid=(rows // MIX_ROWS,),
        in_specs=[pl.BlockSpec((slots, entries), lambda i: (0, 0)), block]
        + [pl.BlockSpec((share, MIX_ROWS, pixel_count), lambda i: (0, i, 0))] * 4
        + [pl.BlockSpec(memory_space=pl.ANY)] * len(before),
        out_specs=[block, pl.BlockSpec((slots, entries), lambda i: (0, 0))],
        out_shape=[
            jax.ShapeDtypeStruct((slots, row_count, pixel_count), bf16),
            jax.ShapeDtypeStruct((slots, entries), f32),
        ],
        input_output_aliases={6: 0} if before else {},
        compiler_params=pltpu.CompilerParams(vmem_limit_bytes=VMEM_LIMIT),
        cost_estimate=COST,
        name="pixel_back",
    )(hyper, pixel_rows, *parts, *before)


def put_kernel(at_ref, *refs, count):
    for j in range(count):

        @pl.when(pl.program_id(0) == j)
        def _(j=j):
            refs[-1][...] = refs[j][...].astype(f32)


def put_parts(pieces, quarters, chunk, chunks, before=()):
    rows, width = pieces[0].shape
    count = len(pieces)
    return pl.pallas_call(
        functools.partial(put_kernel, count=count),
        grid_spec=pltpu.PrefetchScalarGridSpec(
            num_scalar_prefetch=1,
            grid=(count,),
            in_specs=[pl.BlockSpec((rows, width), lambda i, at_ref: (0, 0))] * count
            + [pl.BlockSpec(memory_space=pl.ANY)] * len(before),
            out_specs=pl.BlockSpec((rows, width), lambda i, at_ref: (at_ref[i] * chunks + chunk, 0)),
        ),
        out_shape=jax.ShapeDtypeStruct((4 * chunks * rows, width), f32),
        input_output_aliases={1 + count: 0} if before else {},
        compiler_params=pltpu.CompilerParams(vmem_limit_bytes=VMEM_LIMIT),
        cost_estimate=COST,
        name="put_parts",
    )(jnp.stack(quarters), *pieces, *before)


def take_kernel(quarter_ref, qkv, out_w, fc1, fc2, pieces):
    unit, width = fc2.shape
    for q in range(4):

        @pl.when(quarter_ref[0] == q)
        def _(q=q):
            pieces[0] = out_w[...] if q == 3 else qkv[:, q * width : (q + 1) * width]
            low = fc1[...].astype(f32)
            starts = range(q * unit, fc1.shape[1], 4 * unit)
            pieces[1] = jnp.concatenate([low[:, i : i + unit] for i in starts], axis=1).astype(bf16)

    pieces[2] = fc2[...]


def take_pieces(qkv, out_w, fc1, fc2, quarter):
    rows, width = out_w.shape
    unit = fc2.shape[0] // 4
    whole = lambda i, at: (0, 0)
    return pl.pallas_call(
        take_kernel,
        grid_spec=pltpu.PrefetchScalarGridSpec(
            num_scalar_prefetch=1,
            grid=(1,),
            in_specs=[pl.BlockSpec(array.shape, whole) for array in (qkv, out_w, fc1)]
            + [pl.BlockSpec((unit, width), lambda i, at: (at[0], 0))],
            out_specs=pl.BlockSpec((3, rows, width), lambda i, at: (0, 0, 0)),
        ),
        out_shape=jax.ShapeDtypeStruct((3, rows, width), bf16),
        compiler_params=pltpu.CompilerParams(vmem_limit_bytes=VMEM_LIMIT),
        cost_estimate=COST,
        name="take_pieces",
    )(quarter.reshape(1), qkv, out_w, fc1, fc2)


def give_kernel(order_ref, pieces, qkv, out_w, fc1, fc2):
    unit, width = fc2.shape
    for q in range(4):

        @pl.when(pl.program_id(0) == q)
        def _(q=q):
            piece = pieces[0, 0].astype(f32)
            if q == 3:
                out_w[...] = piece
            else:
                qkv[:, q * width : (q + 1) * width] = piece
            piece = pieces[0, 1].astype(f32)
            for r, i in enumerate(range(q * unit, fc1.shape[1], 4 * unit)):
                fc1[:, i : i + unit] = piece[:, r * unit : (r + 1) * unit]

    fc2[...] = pieces[0, 2].astype(f32)


def give_pieces(pieces, quarter, hidden_width):
    _, _, rows, width = pieces.shape
    unit = rows * hidden_width // (4 * width)
    whole = lambda i, order: (0, 0)
    shapes = [(rows, 3 * width), (rows, width), (rows, hidden_width)]
    return pl.pallas_call(
        give_kernel,
        grid_spec=pltpu.PrefetchScalarGridSpec(
            num_scalar_prefetch=1,
            grid=(4,),
            in_specs=[pl.BlockSpec((1, 3, rows, width), lambda i, order: (order[i], 0, 0, 0))],
            out_specs=[pl.BlockSpec(shape, whole) for shape in shapes]
            + [pl.BlockSpec((unit, width), lambda i, order: (i, 0))],
        ),
        out_shape=[jax.ShapeDtypeStruct(shape, f32) for shape in shapes + [(4 * unit, width)]],
        compiler_params=pltpu.CompilerParams(vmem_limit_bytes=VMEM_LIMIT),
        cost_estimate=COST,
        name="give_pieces",
    )(quarter ^ jnp.arange(4), pieces)


def sum_kernel(left_at, late_at, y_at, left, right, late, left_came, right_came, late_came, *refs):
    to_y, kept_y, kept_x, to_x, scratch = refs
    dx, kind = pl.program_id(0), pl.program_id(1)
    half, shard, _ = to_y.shape[2:]
    lefts = jnp.concatenate([left[0], left_came[0]], axis=0)
    rights = jnp.concatenate([right[0], right_came[0]], axis=0)
    lates = jnp.concatenate([late[0], late_came[0]], axis=0)
    scratch[...] = left_dot(lefts, jnp.where(kind == 0, lates, rights))

    def rows_of(z, y):
        start = pl.multiple_of((2 * z + y) * shard, 8)
        return scratch[pl.ds(start, shard), :].astype(bf16)

    for z in range(half):
        to_y[0, 0, z] = rows_of(z, 1 - y_at[0])
        kept_y[0, 0, z] = rows_of(z, y_at[0])

    def write(out):
        for z in range(half):
            for y in range(2):
                out[0, z, y] = rows_of(half + z, y)

    @pl.when(dx == 0)
    def _():
        write(kept_x)

    @pl.when(dx == 1)
    def _():
        write(to_x)


def sum_blocks(early, late, early_came, late_came, quarter, at_y, z_size):
    _, rows, width = early.shape
    half, kinds = z_size // 2, 3
    shard = width // (2 * z_size)
    low = (2, kinds, half, shard, width)
    high = (kinds, half, 2, shard, width)
    low_spec = pl.BlockSpec((1, 1) + low[2:], lambda d, k, *_: (d, k, 0, 0, 0))
    block = (1, rows, width)
    quarters = jnp.stack([quarter, quarter ^ 2])
    left = pl.BlockSpec(
        block, lambda d, k, left, *_: (jnp.where(k == 0, left[d], jnp.where(k == 1, 2, 4 + d)), 0, 0)
    )
    right = pl.BlockSpec(block, lambda d, k, *_: (jnp.where(k == 2, 3, 6 + d), 0, 0))
    last = pl.BlockSpec(block, lambda d, k, left, late, y: (late[d], 0, 0))
    return pl.pallas_call(
        sum_kernel,
        grid_spec=pltpu.PrefetchScalarGridSpec(
            num_scalar_prefetch=3,
            grid=(2, kinds),
            in_specs=[left, right, last] * 2,
            out_specs=[
                low_spec,
                low_spec,
                pl.BlockSpec((1,) + high[1:], lambda d, k, *_: (jnp.where(d == 0, k, kinds - 1), 0, 0, 0, 0)),
                pl.BlockSpec((1,) + high[1:], lambda d, k, *_: (jnp.where(d == 1, k, 0), 0, 0, 0, 0)),
            ],
            scratch_shapes=[pltpu.VMEM((width, width), f32)],
        ),
        out_shape=[jax.ShapeDtypeStruct(shape, bf16) for shape in (low, low, high, high)],
        compiler_params=pltpu.CompilerParams(vmem_limit_bytes=VMEM_LIMIT),
        cost_estimate=COST,
        name="sum_blocks",
    )(
        jnp.where(quarters == 3, 1, 0),
        quarters,
        at_y.reshape(1),
        early,
        early,
        late,
        early_came,
        early_came,
        late_came,
    )


def pack_kernel(quarter_ref, weight, fc1_bias, *refs, unit):
    vectors, out = refs[:-1], refs[-1]
    lanes = out.shape[1]
    out[0 : weight.shape[0], :] = weight[...]
    row = weight.shape[0]
    fc1_rows = [fc1_bias[pl.ds(quarter_ref[0] ^ q, 1), :] for q in range(4)]
    pieces = [
        fc1_rows[q][:, i : i + unit] for i in range(0, fc1_bias.shape[1], unit) for q in range(4)
    ]
    for vector in [v[...] for v in vectors] + [jnp.concatenate(pieces, axis=1)]:
        for i in range(0, vector.shape[1], lanes):
            out[row : row + 1, :] = vector[:, i : i + lanes]
            row += 1
    out[row:, :] = jnp.zeros((out.shape[0] - row, lanes), f32)


def pack_small(weight, vectors, fc1_bias, unit, quarter):
    lanes = weight.shape[1]
    count = weight.shape[0] + (sum(v.shape[1] for v in vectors) + fc1_bias.size) // lanes
    shape = (-(-count // 8) * 8, lanes)
    whole = lambda i, at: (0, 0)
    arrays = (weight, fc1_bias, *vectors)
    return pl.pallas_call(
        functools.partial(pack_kernel, unit=unit),
        grid_spec=pltpu.PrefetchScalarGridSpec(
            num_scalar_prefetch=1,
            grid=(1,),
            in_specs=[pl.BlockSpec(array.shape, whole) for array in arrays],
            out_specs=pl.BlockSpec(shape, whole),
        ),
        out_shape=jax.ShapeDtypeStruct(shape, f32),
        compiler_params=pltpu.CompilerParams(vmem_limit_bytes=VMEM_LIMIT),
        cost_estimate=COST,
        name="pack_small",
    )(quarter.reshape(1), *arrays)


PAIR = [(0, 1), (1, 0)]
CORNER = [(i, i ^ 3) for i in range(4)]


def swap_core(value):
    return lax.ppermute(value, "c", PAIR)


def swap_x(value):
    return lax.ppermute(value, "x", PAIR)


def swap_y(value):
    return lax.ppermute(value, "y", PAIR)


def swap_plane(values):
    return [
        values[0],
        swap_y(values[1]),
        swap_x(values[2]),
        lax.ppermute(values[3], ("x", "y"), CORNER),
    ]


def after(values, *earlier):
    return lax.optimization_barrier((values, earlier))[0]


def pick(pieces, index):
    return lax.dynamic_index_in_dim(pieces, index, 0, keepdims=False)


UP, DOWN = ([(i, (i + step) % 4) for i in range(4)] for step in (1, 3))


def gather_z_start(own):
    if lax.axis_size("z") != 4:
        return (lax.all_gather(own, "z", axis=0, tiled=False),)
    return lax.ppermute(own, "z", UP), lax.ppermute(own, "z", DOWN)


def gather_z_end(own, came):
    at = lax.axis_index("z")
    if lax.axis_size("z") != 4:
        return came[0]
    half = own.shape[-2] // 2
    below, above = came
    across = [
        lax.ppermute(below[..., :half, :], "z", UP),
        lax.ppermute(above[..., half:, :], "z", DOWN),
    ]
    out = jnp.zeros((4,) + own.shape, own.dtype)
    for piece, step in ((own, 0), (below, 3), (above, 1), (jnp.concatenate(across, axis=-2), 2)):
        out = lax.dynamic_update_index_in_dim(out, piece, (at + step) % 4, 0)
    return out


def scatter_z(pieces):
    size, at = lax.axis_size("z"), lax.axis_index("z")
    if size != 4:
        return lax.psum_scatter(pieces, "z", scatter_dimension=0, tiled=False)
    half = pieces.shape[-2] // 2
    own, above, across, below = (pick(pieces, (at + step) % 4) for step in range(4))
    from_below = lax.ppermute(across[..., :half, :], "z", UP)
    from_above = lax.ppermute(across[..., half:, :], "z", DOWN)
    above = jnp.concatenate([add_low(above[..., :half, :], from_below), above[..., half:, :]], axis=-2)
    below = jnp.concatenate([below[..., :half, :], add_low(below[..., half:, :], from_above)], axis=-2)
    total = own.astype(f32) + lax.ppermute(above, "z", UP).astype(f32)
    return (total + lax.ppermute(below, "z", DOWN).astype(f32)).astype(bf16)


def gather_quarters(own):
    across = swap_x(own)
    return jnp.stack([own, swap_core(own), across, swap_core(across)])


def total_of(value, earlier):
    value = value + swap_core(value)
    value = value + swap_x(value)
    value = value + swap_y(value)
    value = after(value, earlier)
    size, step = lax.axis_size("z"), 1
    while step < size:
        value = value + lax.ppermute(value, "z", [(i, i ^ step) for i in range(size)])
        step *= 2
    return value


def add_low(left, right):
    return (left.astype(f32) + right.astype(f32)).astype(bf16)


def join_y(own, other):
    at_y = lax.axis_index("y")
    both = [jnp.where(at_y == 0, own, other), jnp.where(at_y == 0, other, own)]
    return jnp.stack(both, axis=1).reshape(-1, own.shape[-1])


def gather_start(column):
    half = column.shape[0] // 2
    return swap_y(column[:half]), swap_x(column[half:])


def gather_more(column, came):
    half, kinds = column.shape[0] // 2, column.shape[1]
    low = jnp.stack([join_y(column[:half, kind], came[0][:, kind]) for kind in range(kinds)])
    high = jnp.stack([column[half:], came[1]])
    return low, high


def gather_end(low, high, low_x, high_y):
    return [
        [
            jnp.concatenate([from_low[kind], join_y(high[dx][:, kind], high_y[dx][:, kind])])
            for dx, from_low in enumerate((low, low_x))
        ]
        for kind in range(low.shape[0])
    ]


def sum_more(kept_y, kept_x, from_y, from_x, at_y):
    low = [add_low(kept_y[dx], from_y[dx]) for dx in range(2)]
    high = [
        add_low(*(lax.dynamic_index_in_dim(v, y, 2, False) for v in (kept_x, from_x))) for y in (at_y, 1 - at_y)
    ]
    return low[0], high[0], low[1], high[1]


def sum_end(low, high, low_x, high_y):
    return jnp.concatenate([add_low(low, low_x), add_low(high, high_y)], axis=1).swapaxes(0, 1)


def body(
    pixels,
    wave_table,
    wave_weight,
    wave_bias,
    gen_weight,
    patch_bias,
    norm1_gain,
    norm1_bias,
    qkv_weight,
    query_bias,
    value_bias,
    out_weight,
    out_bias,
    norm2_gain,
    norm2_bias,
    fc1_weight,
    fc1_bias,
    fc2_weight,
    fc2_bias,
    band_count,
    band_table,
    cotangent,
):
    tile_count, seq_len, band_slots, pixel_count = pixels.shape[1:]
    model_width = gen_weight.shape[1]
    wave_width = wave_weight.shape[0]
    hidden_width = fc1_weight.shape[1]
    head_size = model_width // HEADS
    score_scale = head_size ** (-0.5)
    row_count = tile_count * seq_len
    head_shape = (tile_count, seq_len, HEADS, head_size)
    z_size = lax.axis_size("z")
    row_size = 2 * z_size
    at_x, at_c, at_y = lax.axis_index("x"), lax.axis_index("c"), lax.axis_index("y")
    quarter = 2 * at_x + at_c
    shard = qkv_weight.shape[0]
    unit = hidden_width // row_size // 4

    gen_rows = gen_weight.shape[0] // 4
    own_rows = lax.dynamic_slice_in_dim(gen_weight, quarter * gen_rows, gen_rows, 0)
    gen = lax.all_gather(own_rows, ("c", "z"), axis=0, tiled=True).reshape(-1, pixel_count, model_width)

    unit_order = fc1_bias.reshape(row_size, 4, unit).transpose(1, 0, 2).reshape(4, row_size * unit)
    bias_fc1 = [pick(unit_order, quarter ^ d) for d in range(4)]

    onehot = (band_table[0][:, None] == jnp.arange(wave_table.shape[0])[None, :]).astype(f32)
    wavelength = jnp.dot(onehot, wave_table, precision=highest)
    wave_embed = sincos(wavelength * 1000.0, wave_width)
    live = (jnp.arange(band_slots) < band_count[0]).astype(f32)[:, None]

    def hyper_fn(weight, bias):
        return jax.nn.gelu(jnp.dot(wave_embed, weight, precision=highest) + bias) * live

    hyper, hyper_back = jax.vjp(hyper_fn, wave_weight.astype(f32), wave_bias)
    per_row = wave_width // row_size
    place = jnp.arange(wave_width)
    kk = place % (per_row // 4)
    place = place // (per_row // 4)
    entry_z = place % z_size
    place = place // z_size
    entry_c, entry_y, entry_x = place % 2, (place // 2 % 2) ^ at_y, (place // 4) ^ at_x
    entry = per_row * (2 * entry_z + entry_y) + per_row // 4 * (2 * entry_x + entry_c) + kk
    order = (jnp.arange(wave_width)[:, None] == entry[None, :]).astype(bf16)
    hyper_low = dense_dot(hyper.astype(bf16), order).astype(bf16)

    pixel_rows = pixels.reshape(row_count, band_slots, pixel_count).transpose(1, 0, 2)
    mixed_pixels = mix_pixels(hyper_low.T, pixel_rows)
    patches = swap_plane(mixed_pixels)

    weights = after((qkv_weight, out_weight, fc1_weight, fc2_weight), mixed_pixels)
    own_pieces = take_pieces(*weights, quarter)
    column = gather_z_end(own_pieces, gather_z_start(own_pieces))
    column, patches = after((column, patches))
    column_came = gather_start(column)
    low, high = gather_more(column, column_came)
    attn, fc = (low[:1], high[:, :, :1]), (low[1:], high[:, :, 1:])
    attn_came = swap_x(attn[0]), swap_y(attn[1])
    attn_came, fc = after((attn_came, fc))
    fc_came = swap_x(fc[0]), swap_y(fc[1])

    def both_cores(blocks):
        return [block for owned in blocks for block in (owned, swap_core(owned))]

    attn = jnp.stack(both_cores(gather_end(*attn, *attn_came)[0]))
    gen = after(gen, attn_came)
    partial = project(patches, gen)
    partial = [partial[j * row_count : (j + 1) * row_count] for j in range(4)]
    partial = [partial[0]] + swap_plane([piece.astype(bf16) for piece in partial])[1:]
    projected = (partial[0] + partial[1]) + (partial[2] + partial[3])
    fc_came = after(fc_came, projected)
    w_query, w_key, w_value, w_out = (pick(attn, j ^ quarter) for j in range(4))
    position = sincos(jnp.arange(seq_len).astype(f32), model_width)
    embedded = (projected + patch_bias).reshape(tile_count, seq_len, model_width) + position
    embedded = embedded.reshape(row_count, model_width)

    normed = layer_norm(embedded, norm1_gain, norm1_bias).astype(bf16)
    queries = (dense_dot(normed, w_query) + query_bias).astype(bf16).reshape(head_shape)
    key_rows = dense_dot(normed, w_key).astype(bf16).reshape(head_shape)
    value_rows = (dense_dot(normed, w_value) + value_bias).astype(bf16).reshape(head_shape)
    scores = (
        jnp.einsum("tqhd,tkhd->thqk", queries, key_rows, preferred_element_type=f32) * score_scale
    )
    probs_full = jax.nn.softmax(scores, axis=-1)
    probs = probs_full.astype(bf16)
    attended = (
        jnp.einsum("thqk,tkhd->tqhd", probs, value_rows, preferred_element_type=f32)
        .astype(bf16)
        .reshape(row_count, model_width)
    )
    middle = embedded + dense_dot(attended, w_out) + out_bias
    fc_came = after(fc_came, middle)
    w_fc1, w_fc2 = (both_cores(blocks) for blocks in gather_end(*fc, *fc_came))
    other_patches = [swap_core(part) for part in after(patches, middle)]
    normed_two = layer_norm(middle, norm2_gain, norm2_bias).astype(bf16)
    fc_pre = [dense_dot(normed_two, w) + bias for w, bias in zip(w_fc1, bias_fc1)]
    hidden, gelu_back = zip(*(jax.vjp(jax.nn.gelu, values) for values in fc_pre))
    hidden = [values.astype(bf16) for values in hidden]
    block_out = middle + sum(dense_dot(values, w) for values, w in zip(hidden, w_fc2)) + fc2_bias

    grad_out = cotangent.reshape(row_count, model_width)
    fc2_bias_part = row_total(grad_out)
    grad_pre = [
        back(right_dot(grad_out, w))[0].astype(bf16) for back, w in zip(gelu_back, w_fc2)
    ]
    fc1_bias_part = jnp.concatenate([row_total(values) for values in grad_pre])
    common = [normed, attended, normed_two, grad_out]
    early_values = jnp.stack(common + [hidden[0], hidden[2], grad_pre[0], grad_pre[2]])
    early_came = swap_core(jnp.stack(common + [hidden[1], hidden[3], grad_pre[1], grad_pre[3]]))
    grad_normed_two = sum(right_dot(values, w) for values, w in zip(grad_pre, w_fc1))
    norm_two_back = jax.vjp(layer_norm, middle, norm2_gain, norm2_bias)[1]
    grad_middle, norm2_gain_part, norm2_bias_part = norm_two_back(grad_normed_two)
    grad_middle = grad_middle + grad_out.astype(f32)
    grad_branch = grad_middle.astype(bf16)
    out_bias_part = row_total(grad_branch)
    grad_attended = right_dot(grad_branch, w_out).astype(bf16).reshape(head_shape)
    grad_probs = jnp.einsum(
        "tqhd,tkhd->thqk", grad_attended, value_rows, preferred_element_type=f32
    )
    grad_scores = probs_full * (
        grad_probs - jnp.sum(probs_full * grad_probs, axis=-1, keepdims=True)
    )
    grad_scores = grad_scores.astype(bf16)
    grad_queries = (
        jnp.einsum("thqk,tkhd->tqhd", grad_scores, key_rows, preferred_element_type=f32)
        * score_scale
    ).astype(bf16)
    grad_keys = (
        jnp.einsum("thqk,tqhd->tkhd", grad_scores, queries, preferred_element_type=f32)
        * score_scale
    ).astype(bf16)
    grad_values = jnp.einsum(
        "thqk,tqhd->tkhd", probs, grad_attended, preferred_element_type=f32
    ).astype(bf16)
    grad_queries = grad_queries.reshape(row_count, model_width)
    grad_values = grad_values.reshape(row_count, model_width)
    grad_keys = grad_keys.reshape(row_count, model_width)
    query_bias_part = row_total(grad_queries)
    value_bias_part = row_total(grad_values)
    grad_normed = right_dot(grad_queries, w_query)
    grad_normed += right_dot(grad_keys, w_key)
    grad_normed += right_dot(grad_values, w_value)
    grad_normed, early_came, other_patches = after((grad_normed, early_came, other_patches))
    norm_one_back = jax.vjp(layer_norm, embedded, norm1_gain, norm1_bias)[1]
    grad_from_norm, norm1_gain_part, norm1_bias_part = norm_one_back(grad_normed)
    grad_embedded = (grad_middle + grad_from_norm).astype(bf16)
    patch_bias_part = row_total(grad_embedded)

    grads = swap_plane([grad_embedded] * 4)
    early = early_rows(row_count)
    back_early = back_patches(grads, gen, 0, early)
    grads, back_early = after((grads, back_early))
    back_early = swap_plane(back_early)
    other_grads = swap_core(jnp.concatenate(grads))
    chunks = 2 if wave_width // row_size // 4 == GEN_STEP else 1
    gen_sent = gen_grad(patches, other_patches, grads, other_grads, chunks, at_c)
    gen_parts = [
        lax.psum_scatter(chunk.reshape(-1, model_width), "z", scatter_dimension=0, tiled=True)
        for chunk in gen_sent
    ]

    late_values = jnp.stack([grad_queries, grad_keys, grad_values, grad_branch])
    late_came = swap_core(late_values)
    to_y, kept_y, kept_x, to_x = sum_blocks(
        early_values, late_values, early_came, late_came, quarter, at_y, z_size
    )
    back_late = back_patches(after(grads, gen_sent), gen, early, row_count - early)
    to_y, to_x, back_early, back_late = after((to_y, to_x, back_early, back_late))
    back_late = swap_plane(back_late)
    from_y, from_x = swap_y(to_y), swap_x(to_x)
    pixel_grad, hyper_early = pixel_back(hyper_low, pixel_rows, back_early, 0)
    back_late, from_y, from_x, hyper_early = after((back_late, from_y, from_x, hyper_early))
    low, high, low_sent, high_sent = sum_more(kept_y, kept_x, from_y, from_x, at_y)
    low_x, high_y = swap_x(low_sent), swap_y(high_sent)
    pixel_grad, hyper_late = pixel_back(hyper_low, pixel_rows, back_late, early, (pixel_grad,))
    low_x, high_y, hyper_late, gen_parts = after((low_x, high_y, hyper_late, gen_parts))
    across = [swap_x(piece) for piece in gen_parts]
    gen_total = ()
    for chunk, piece in enumerate(gen_parts):
        pair = piece, swap_core(piece)
        gen_total = (put_parts(pair, (quarter, quarter ^ 1), chunk, chunks, gen_total),)
    share_sum = scatter_z(sum_end(low, high, low_x, high_y))
    qkv_total, out_total, fc1_total, fc2_total = give_pieces(gather_quarters(share_sum), quarter, hidden_width)

    grad_hyper = hyper_early + hyper_late
    grad_hyper = lax.dot_general(
        grad_hyper, order.astype(f32), (((1,), (1,)), ((), ())), precision=highest
    )
    wave_weight_part, wave_bias_part = hyper_back(grad_hyper)
    norm_parts = [norm1_gain_part, norm1_bias_part, norm2_gain_part, norm2_bias_part, wave_bias_part]
    norm_parts = [part.reshape(1, -1) for part in norm_parts]
    small = [*norm_parts, patch_bias_part, query_bias_part, value_bias_part, out_bias_part, fc2_bias_part]
    cuts = np.cumsum([part.shape[1] for part in small] + [hidden_width])
    small = pack_small(wave_weight_part, small, fc1_bias_part, unit, quarter)
    small = total_of(small, (share_sum, gen_total))
    for chunk, piece in enumerate(across):
        pair = piece, swap_core(piece)
        gen_total = (put_parts(pair, (quarter ^ 2, quarter ^ 3), chunk, chunks, gen_total),)
    gen_total = gen_total[0]
    wave_weight_total, small = small[:wave_width], small[wave_width:].reshape(-1)
    (
        norm1_gain_total,
        norm1_bias_total,
        norm2_gain_total,
        norm2_bias_total,
        wave_bias_total,
        patch_bias_total,
        query_bias_total,
        value_bias_total,
        out_bias_total,
        fc2_bias_total,
        fc1_bias_total,
        _,
    ) = jnp.split(small, cuts)
    block_result = block_out.astype(bf16).reshape(1, tile_count, seq_len, model_width)
    pixel_result = pixel_grad.transpose(1, 0, 2).reshape(1, tile_count, seq_len, band_slots, pixel_count)
    return (
        block_result,
        pixel_result,
        wave_weight_total,
        wave_bias_total,
        gen_total,
        patch_bias_total,
        norm1_gain_total,
        norm1_bias_total,
        qkv_total,
        query_bias_total,
        value_bias_total,
        out_total,
        out_bias_total,
        norm2_gain_total,
        norm2_bias_total,
        fc1_total,
        fc1_bias_total,
        fc2_total,
        fc2_bias_total,
    )


def row_sum(values):
    return jnp.sum(values.astype(f32), axis=0)


def general_body(
    pixels,
    wave_table,
    wave_weight,
    wave_bias,
    gen_weight,
    patch_bias,
    norm1_gain,
    norm1_bias,
    qkv_weight,
    query_bias,
    value_bias,
    out_weight,
    out_bias,
    norm2_gain,
    norm2_bias,
    fc1_weight,
    fc1_bias,
    fc2_weight,
    fc2_bias,
    band_count,
    band_table,
    cotangent,
):
    tile_count, seq_len, band_slots, pixel_count = pixels.shape[1:]
    model_width = gen_weight.shape[1]
    wave_width = wave_weight.shape[0]
    head_size = model_width // HEADS
    score_scale = head_size ** (-0.5)
    row_count = tile_count * seq_len
    head_shape = (tile_count, seq_len, HEADS, head_size)
    pixel_rows = pixels.reshape(row_count, band_slots, pixel_count)
    onehot = (band_table[0][:, None] == jnp.arange(wave_table.shape[0])[None, :]).astype(
        f32
    )
    wavelength = jnp.dot(onehot, wave_table, precision=highest)
    wave_embed = sincos(wavelength * 1000.0, wave_width)
    live = (jnp.arange(band_slots) < band_count[0]).astype(f32)[:, None]

    def hyper_fn(weight, bias):
        return jax.nn.gelu(jnp.dot(wave_embed, weight, precision=highest) + bias) * live

    hyper, hyper_back = jax.vjp(hyper_fn, wave_weight.astype(f32), wave_bias)
    hyper_low = hyper.astype(bf16)
    patches = jnp.einsum("bk,rbp->rkp", hyper_low, pixel_rows, preferred_element_type=f32)
    patches = patches.astype(bf16).reshape(row_count, wave_width * pixel_count)
    position = sincos(jnp.arange(seq_len).astype(f32), model_width)
    columns = patches
    projected = dense_dot(columns, lax.all_gather(gen_weight, "row", axis=0, tiled=True))
    embedded = (projected + patch_bias).reshape(tile_count, seq_len, model_width) + position
    embedded = embedded.reshape(row_count, model_width)
    w_qkv, w_out, w_fc1, w_fc2 = (
        lax.all_gather(qkv_weight, "row", axis=0, tiled=True),
        lax.all_gather(out_weight, "row", axis=0, tiled=True),
        lax.all_gather(fc1_weight, "row", axis=0, tiled=True),
        lax.all_gather(fc2_weight, "row", axis=0, tiled=True),
    )

    def front(inputs):
        normed = layer_norm(inputs, norm1_gain, norm1_bias).astype(bf16)
        mixed = dense_dot(normed, w_qkv)
        queries = (mixed[:, :model_width] + query_bias).astype(bf16).reshape(head_shape)
        key_rows = mixed[:, model_width : 2 * model_width].astype(bf16).reshape(head_shape)
        value_rows = (
            (mixed[:, 2 * model_width :] + value_bias).astype(bf16).reshape(head_shape)
        )
        return (normed, queries, key_rows, value_rows)

    def scores_of(queries, key_rows):
        return (
            jnp.einsum("tqhd,tkhd->thqk", queries, key_rows, preferred_element_type=f32)
            * score_scale
        )

    def attend(probs, value_rows):
        mixed_heads = jnp.einsum(
            "thqk,tkhd->tqhd", probs, value_rows, preferred_element_type=f32
        )
        return mixed_heads.astype(bf16).reshape(row_count, model_width)

    def back_half(inputs, attended):
        middle = inputs + dense_dot(attended, w_out) + out_bias
        normed_two = layer_norm(middle, norm2_gain, norm2_bias).astype(bf16)
        fc_pre = dense_dot(normed_two, w_fc1) + fc1_bias
        hidden = jax.nn.gelu(fc_pre).astype(bf16)
        return (middle, normed_two, fc_pre, hidden)

    normed, queries, key_rows, value_rows = front(embedded)
    scores = scores_of(queries, key_rows)
    log_total = jax.nn.logsumexp(scores, axis=-1, keepdims=True)
    attended = attend(jnp.exp(scores - log_total).astype(bf16), value_rows)
    middle, normed_two, fc_pre, hidden = back_half(embedded, attended)
    block_out = middle + dense_dot(hidden, w_fc2) + fc2_bias
    grad_out = cotangent.reshape(row_count, model_width)
    normed, queries, key_rows, value_rows = front(embedded)
    probs_full = jnp.exp(scores_of(queries, key_rows) - log_total)
    probs = probs_full.astype(bf16)
    attended = attend(probs, value_rows)
    middle, normed_two, fc_pre, hidden = back_half(embedded, attended)
    fc2_bias_part = row_sum(grad_out)
    fc2_grad = left_dot(hidden, grad_out)
    grad_hidden = right_dot(grad_out, w_fc2)
    grad_pre = jax.vjp(jax.nn.gelu, fc_pre)[1](grad_hidden)[0].astype(bf16)
    fc1_bias_part = row_sum(grad_pre)
    fc1_grad = left_dot(normed_two, grad_pre)
    grad_normed_two = right_dot(grad_pre, w_fc1)
    norm_two_back = jax.vjp(layer_norm, middle, norm2_gain, norm2_bias)[1]
    grad_middle, norm2_gain_part, norm2_bias_part = norm_two_back(grad_normed_two)
    grad_middle = grad_middle + grad_out.astype(f32)
    grad_branch = grad_middle.astype(bf16)
    out_bias_part = row_sum(grad_branch)
    out_grad = left_dot(attended, grad_branch)
    grad_attended = right_dot(grad_branch, w_out).astype(bf16).reshape(head_shape)
    grad_probs = jnp.einsum(
        "tqhd,tkhd->thqk", grad_attended, value_rows, preferred_element_type=f32
    )
    grad_scores = probs_full * (
        grad_probs - jnp.sum(probs_full * grad_probs, axis=-1, keepdims=True)
    )
    grad_scores = grad_scores.astype(bf16)
    grad_queries = (
        jnp.einsum("thqk,tkhd->tqhd", grad_scores, key_rows, preferred_element_type=f32)
        * score_scale
    ).astype(bf16)
    grad_keys = (
        jnp.einsum("thqk,tqhd->tkhd", grad_scores, queries, preferred_element_type=f32)
        * score_scale
    ).astype(bf16)
    grad_values = jnp.einsum(
        "thqk,tqhd->tkhd", probs, grad_attended, preferred_element_type=f32
    ).astype(bf16)
    grad_queries = grad_queries.reshape(row_count, model_width)
    grad_values = grad_values.reshape(row_count, model_width)
    grad_mixed = jnp.concatenate(
        [grad_queries, grad_keys.reshape(row_count, model_width), grad_values], axis=1
    )
    query_bias_part = row_sum(grad_queries)
    value_bias_part = row_sum(grad_values)
    qkv_grad = left_dot(normed, grad_mixed)
    grad_normed = right_dot(grad_mixed, w_qkv)
    norm_one_back = jax.vjp(layer_norm, embedded, norm1_gain, norm1_bias)[1]
    grad_from_norm, norm1_gain_part, norm1_bias_part = norm_one_back(grad_normed)
    grad_embedded = (grad_middle + grad_from_norm).astype(bf16)
    patch_bias_part = row_sum(grad_embedded)
    grad_patches = right_dot(
        grad_embedded, lax.all_gather(gen_weight, "row", axis=0, tiled=True)
    ).astype(bf16)
    grad_cube = grad_patches.reshape(row_count, wave_width, pixel_count)
    pixel_grad = jnp.einsum(
        "rkp,bk->rbp", grad_cube, hyper_low, preferred_element_type=f32
    ).astype(bf16)
    grad_hyper = jnp.einsum(
        "rkp,rbp->bk", grad_cube, pixel_rows, preferred_element_type=f32
    )
    wave_weight_part, wave_bias_part = hyper_back(grad_hyper)
    columns = patches
    gen_part = lax.psum_scatter(
        left_dot(columns, grad_embedded), "row", scatter_dimension=0, tiled=True
    )
    qkv_share, out_share, fc1_share, fc2_share = (
        lax.psum_scatter(qkv_grad, "row", scatter_dimension=0, tiled=True),
        lax.psum_scatter(out_grad, "row", scatter_dimension=0, tiled=True),
        lax.psum_scatter(fc1_grad, "row", scatter_dimension=0, tiled=True),
        lax.psum_scatter(fc2_grad, "row", scatter_dimension=0, tiled=True),
    )
    gen_total, qkv_total, out_total, fc1_total, fc2_total = (
        lax.psum(gen_part.astype(bf16), "grp").astype(f32),
        lax.psum(qkv_share.astype(bf16), "grp").astype(f32),
        lax.psum(out_share.astype(bf16), "grp").astype(f32),
        lax.psum(fc1_share.astype(bf16), "grp").astype(f32),
        lax.psum(fc2_share.astype(bf16), "grp").astype(f32),
    )
    small_totals = lax.psum(
        (
            wave_weight_part,
            wave_bias_part,
            patch_bias_part,
            norm1_gain_part,
            norm1_bias_part,
            query_bias_part,
            value_bias_part,
            out_bias_part,
            norm2_gain_part,
            norm2_bias_part,
            fc1_bias_part,
            fc2_bias_part,
        ),
        ("grp", "row"),
    )
    (
        wave_weight_total,
        wave_bias_total,
        patch_bias_total,
        norm1_gain_total,
        norm1_bias_total,
        query_bias_total,
        value_bias_total,
        out_bias_total,
        norm2_gain_total,
        norm2_bias_total,
        fc1_bias_total,
        fc2_bias_total,
    ) = small_totals
    block_result = block_out.astype(bf16).reshape(1, tile_count, seq_len, model_width)
    pixel_result = pixel_grad.reshape(1, tile_count, seq_len, band_slots, pixel_count)
    return (
        block_result,
        pixel_result,
        wave_weight_total,
        wave_bias_total,
        gen_total,
        patch_bias_total,
        norm1_gain_total,
        norm1_bias_total,
        qkv_total,
        query_bias_total,
        value_bias_total,
        out_total,
        out_bias_total,
        norm2_gain_total,
        norm2_bias_total,
        fc1_total,
        fc1_bias_total,
        fc2_total,
        fc2_bias_total,
    )


def solution(mesh):
    grp_size, row_size = mesh.devices.shape
    if (grp_size, row_size) == PLANNED:
        step, grp, row = body, ("x", "c"), ("z", "y")
        mesh = Mesh(mesh.devices.reshape(grp_size // 2, 2, row_size // 2, 2), AXES)
    else:
        step, grp, row = general_body, "grp", "row"
    return jax.shard_map(
        step,
        mesh=mesh,
        in_specs=(
            P(grp, row, None, None, None),
            P(),
            P(),
            P(),
            P(row, None),
            P(),
            P(),
            P(),
            P(row, None),
            P(),
            P(),
            P(row, None),
            P(),
            P(),
            P(),
            P(row, None),
            P(),
            P(row, None),
            P(),
            P(grp),
            P(grp, None),
            P(grp, row, None, None),
        ),
        out_specs=(
            P(grp, row, None, None),
            P(grp, row, None, None, None),
            P(),
            P(),
            P(row, None),
            P(),
            P(),
            P(),
            P(row, None),
            P(),
            P(),
            P(row, None),
            P(),
            P(),
            P(),
            P(row, None),
            P(),
            P(row, None),
            P(),
        ),
        check_vma=False,
    )
```

```python
import functools

import jax
import jax.numpy as jnp
import numpy as np
from jax import lax
from jax.experimental import pallas as pl
from jax.experimental.pallas import tpu as pltpu
from jax.sharding import Mesh
from jax.sharding import PartitionSpec as P

HEADS = 12

bf16 = jnp.bfloat16
f32 = jnp.float32
highest = lax.Precision.HIGHEST
epsilon = 1e-06

AXES = ("x", "c", "z", "y")
PLANNED = (4, 8)
VMEM_LIMIT = 48 * 1024 * 1024
MIX_ROWS = 32
GEN_STEP = 4
COST = pl.CostEstimate(flops=1, bytes_accessed=1, transcendentals=0)


def sincos(angles_in, out_width):
    half_width = out_width // 2
    freqs = 1.0 / 10000.0 ** (jnp.arange(half_width).astype(angles_in.dtype) * (2.0 / out_width))
    angles = angles_in[:, None] * freqs[None, :]
    return jnp.concatenate([jnp.sin(angles), jnp.cos(angles)], axis=1)


def layer_norm(inputs, gain, shift):
    center = inputs - jnp.mean(inputs, axis=-1, keepdims=True)
    spread = jnp.mean(center * center, axis=-1, keepdims=True)
    return center * lax.rsqrt(spread + epsilon) * gain + shift


def dense_dot(left, right):
    return jnp.dot(left, right, preferred_element_type=f32)


def left_dot(left, right):
    return lax.dot_general(left, right, (((0,), (0,)), ((), ())), preferred_element_type=f32)


def right_dot(left, right):
    return lax.dot_general(left, right, (((1,), (1,)), ((), ())), preferred_element_type=f32)


def row_total(values):
    return jnp.sum(values.astype(f32), axis=0, keepdims=True)


def mix_kernel(hyper_ref, pix_ref, *outs):
    slots, rows, pixel_count = pix_ref.shape
    entries = hyper_ref.shape[0]
    mixed = dense_dot(hyper_ref[...], pix_ref[...].reshape(slots, rows * pixel_count))
    mixed = mixed.astype(bf16).reshape(entries, rows, pixel_count)
    for j, out in enumerate(outs):
        share = out.shape[0]
        out[...] = mixed[j * share : (j + 1) * share]


def mix_pixels(hyper_t, pixel_rows):
    entries = hyper_t.shape[0]
    slots, row_count, pixel_count = pixel_rows.shape
    share = entries // 4
    out = jax.ShapeDtypeStruct((share, row_count, pixel_count), bf16)
    return pl.pallas_call(
        mix_kernel,
        grid=(row_count // MIX_ROWS,),
        in_specs=[
            pl.BlockSpec((entries, slots), lambda i: (0, 0)),
            pl.BlockSpec((slots, MIX_ROWS, pixel_count), lambda i: (0, i, 0)),
        ],
        out_specs=[pl.BlockSpec((share, MIX_ROWS, pixel_count), lambda i: (0, i, 0))] * 4,
        out_shape=[out] * 4,
        compiler_params=pltpu.CompilerParams(vmem_limit_bytes=VMEM_LIMIT),
        cost_estimate=COST,
        name="mix_pixels",
    )(hyper_t, pixel_rows)


def project_kernel(a0, a1, a2, a3, w, out):
    @pl.when(pl.program_id(0) == 0)
    def _():
        out[...] = jnp.zeros_like(out)

    for k in range(w.shape[0]):
        left = jnp.concatenate([a[k] for a in (a0, a1, a2, a3)], axis=0)
        out[...] += dense_dot(left, w[k])


def project(parts, gen):
    share, rows, pixel_count = parts[0].shape
    width = gen.shape[2]
    return pl.pallas_call(
        project_kernel,
        grid=(share // GEN_STEP,),
        in_specs=[pl.BlockSpec((GEN_STEP, rows, pixel_count), lambda i: (i, 0, 0))] * 4
        + [pl.BlockSpec((GEN_STEP, pixel_count, width), lambda i: (i, 0, 0))],
        out_specs=pl.BlockSpec((4 * rows, width), lambda i: (0, 0)),
        out_shape=jax.ShapeDtypeStruct((4 * rows, width), f32),
        compiler_params=pltpu.CompilerParams(vmem_limit_bytes=VMEM_LIMIT),
        cost_estimate=COST,
        name="project",
    )(*parts, gen)


def early_rows(rows):
    return rows // 4 * 3


def back_kernel(g0, g1, g2, g3, w, *outs):
    rows = g0.shape[0]
    grads = jnp.concatenate([g[...] for g in (g0, g1, g2, g3)], axis=0)
    for k in range(w.shape[0]):
        res = right_dot(grads, w[k]).astype(bf16)
        for j, out in enumerate(outs):
            out[k] = res[j * rows : (j + 1) * rows]


def back_patches(grads, gen, start, rows):
    share, pixel_count, width = gen.shape
    return pl.pallas_call(
        back_kernel,
        grid=(share // GEN_STEP,),
        in_specs=[pl.BlockSpec((rows, width), lambda i: (start // rows, 0))] * 4
        + [pl.BlockSpec((GEN_STEP, pixel_count, width), lambda i: (i, 0, 0))],
        out_specs=[pl.BlockSpec((GEN_STEP, rows, pixel_count), lambda i: (i, 0, 0))] * 4,
        out_shape=[jax.ShapeDtypeStruct((share, rows, pixel_count), bf16)] * 4,
        compiler_params=pltpu.CompilerParams(vmem_limit_bytes=VMEM_LIMIT),
        cost_estimate=COST,
        name="back_patches",
    )(*grads, gen)


def gen_grad_kernel(core_ref, *refs):
    parts, grad_refs, outs = refs[:8], refs[8:13], refs[13:]
    grads = jnp.concatenate([g[...] for g in grad_refs], axis=0)
    cut = outs[0].shape[1]
    for k in range(cut * len(outs)):
        left = jnp.concatenate([a[k] for a in parts], axis=0)
        outs[k // cut][0, k % cut] = left_dot(left, grads).astype(bf16)


def gen_grad(parts, others, grads, other_grads, chunks, at_c):
    share, rows, pixel_count = others[0].shape
    width = other_grads.shape[1]
    steps = share // 2 // GEN_STEP
    cut = GEN_STEP // chunks
    block = (GEN_STEP, rows, pixel_count)
    return pl.pallas_call(
        gen_grad_kernel,
        grid_spec=pltpu.PrefetchScalarGridSpec(
            num_scalar_prefetch=1,
            grid=(steps,),
            in_specs=[pl.BlockSpec(block, lambda i, core: (core[0] * steps + i, 0, 0))] * 8
            + [pl.BlockSpec((rows, width), lambda i, core: (0, 0))] * 4
            + [pl.BlockSpec((4 * rows, width), lambda i, core: (0, 0))],
            out_specs=[pl.BlockSpec((1, cut, pixel_count, width), lambda i, core: (i, 0, 0, 0))] * chunks,
        ),
        out_shape=[jax.ShapeDtypeStruct((steps, cut, pixel_count, width), bf16)] * chunks,
        compiler_params=pltpu.CompilerParams(vmem_limit_bytes=VMEM_LIMIT),
        cost_estimate=COST,
        name="gen_grad",
    )(at_c.reshape(1), *parts, *others, *grads, other_grads)


def pixel_kernel(hyper_ref, pix_ref, g0, g1, g2, g3, *refs):
    grad_ref, total_ref = refs[-2:]
    slots, rows, pixel_count = pix_ref.shape
    entries = hyper_ref.shape[1]

    @pl.when(pl.program_id(0) == 0)
    def _():
        total_ref[...] = jnp.zeros_like(total_ref)

    grad = jnp.concatenate([g[...] for g in (g0, g1, g2, g3)], axis=0)
    grad = grad.reshape(entries, rows * pixel_count)
    pix = pix_ref[...].reshape(slots, rows * pixel_count)
    out = dense_dot(hyper_ref[...], grad).astype(bf16)
    grad_ref[...] = out.reshape(slots, rows, pixel_count)
    total_ref[...] += right_dot(pix, grad)


def pixel_back(hyper, pixel_rows, parts, start, before=()):
    slots, entries = hyper.shape
    _, row_count, pixel_count = pixel_rows.shape
    share, rows, _ = parts[0].shape
    block = pl.BlockSpec((slots, MIX_ROWS, pixel_count), lambda i: (0, start // MIX_ROWS + i, 0))
    return pl.pallas_call(
        pixel_kernel,
        grid=(rows // MIX_ROWS,),
        in_specs=[pl.BlockSpec((slots, entries), lambda i: (0, 0)), block]
        + [pl.BlockSpec((share, MIX_ROWS, pixel_count), lambda i: (0, i, 0))] * 4
        + [pl.BlockSpec(memory_space=pl.ANY)] * len(before),
        out_specs=[block, pl.BlockSpec((slots, entries), lambda i: (0, 0))],
        out_shape=[
            jax.ShapeDtypeStruct((slots, row_count, pixel_count), bf16),
            jax.ShapeDtypeStruct((slots, entries), f32),
        ],
        input_output_aliases={6: 0} if before else {},
        compiler_params=pltpu.CompilerParams(vmem_limit_bytes=VMEM_LIMIT),
        cost_estimate=COST,
        name="pixel_back",
    )(hyper, pixel_rows, *parts, *before)


def put_kernel(at_ref, *refs, count):
    for j in range(count):

        @pl.when(pl.program_id(0) == j)
        def _(j=j):
            refs[-1][...] = refs[j][...].astype(f32)


def put_parts(pieces, quarters, chunk, chunks, before=()):
    rows, width = pieces[0].shape
    count = len(pieces)
    return pl.pallas_call(
        functools.partial(put_kernel, count=count),
        grid_spec=pltpu.PrefetchScalarGridSpec(
            num_scalar_prefetch=1,
            grid=(count,),
            in_specs=[pl.BlockSpec((rows, width), lambda i, at_ref: (0, 0))] * count
            + [pl.BlockSpec(memory_space=pl.ANY)] * len(before),
            out_specs=pl.BlockSpec((rows, width), lambda i, at_ref: (at_ref[i] * chunks + chunk, 0)),
        ),
        out_shape=jax.ShapeDtypeStruct((4 * chunks * rows, width), f32),
        input_output_aliases={1 + count: 0} if before else {},
        compiler_params=pltpu.CompilerParams(vmem_limit_bytes=VMEM_LIMIT),
        cost_estimate=COST,
        name="put_parts",
    )(jnp.stack(quarters), *pieces, *before)


def take_kernel(quarter_ref, qkv, out_w, fc1, fc2, pieces):
    unit, width = fc2.shape
    for q in range(4):

        @pl.when(quarter_ref[0] == q)
        def _(q=q):
            pieces[0] = out_w[...] if q == 3 else qkv[:, q * width : (q + 1) * width]
            low = fc1[...].astype(f32)
            starts = range(q * unit, fc1.shape[1], 4 * unit)
            pieces[1] = jnp.concatenate([low[:, i : i + unit] for i in starts], axis=1).astype(bf16)

    pieces[2] = fc2[...]


def take_pieces(qkv, out_w, fc1, fc2, quarter):
    rows, width = out_w.shape
    unit = fc2.shape[0] // 4
    whole = lambda i, at: (0, 0)
    return pl.pallas_call(
        take_kernel,
        grid_spec=pltpu.PrefetchScalarGridSpec(
            num_scalar_prefetch=1,
            grid=(1,),
            in_specs=[pl.BlockSpec(array.shape, whole) for array in (qkv, out_w, fc1)]
            + [pl.BlockSpec((unit, width), lambda i, at: (at[0], 0))],
            out_specs=pl.BlockSpec((3, rows, width), lambda i, at: (0, 0, 0)),
        ),
        out_shape=jax.ShapeDtypeStruct((3, rows, width), bf16),
        compiler_params=pltpu.CompilerParams(vmem_limit_bytes=VMEM_LIMIT),
        cost_estimate=COST,
        name="take_pieces",
    )(quarter.reshape(1), qkv, out_w, fc1, fc2)


def give_kernel(order_ref, pieces, qkv, out_w, fc1, fc2):
    unit, width = fc2.shape
    for q in range(4):

        @pl.when(pl.program_id(0) == q)
        def _(q=q):
            piece = pieces[0, 0].astype(f32)
            if q == 3:
                out_w[...] = piece
            else:
                qkv[:, q * width : (q + 1) * width] = piece
            piece = pieces[0, 1].astype(f32)
            for r, i in enumerate(range(q * unit, fc1.shape[1], 4 * unit)):
                fc1[:, i : i + unit] = piece[:, r * unit : (r + 1) * unit]

    fc2[...] = pieces[0, 2].astype(f32)


def give_pieces(pieces, quarter, hidden_width):
    _, _, rows, width = pieces.shape
    unit = rows * hidden_width // (4 * width)
    whole = lambda i, order: (0, 0)
    shapes = [(rows, 3 * width), (rows, width), (rows, hidden_width)]
    return pl.pallas_call(
        give_kernel,
        grid_spec=pltpu.PrefetchScalarGridSpec(
            num_scalar_prefetch=1,
            grid=(4,),
            in_specs=[pl.BlockSpec((1, 3, rows, width), lambda i, order: (order[i], 0, 0, 0))],
            out_specs=[pl.BlockSpec(shape, whole) for shape in shapes]
            + [pl.BlockSpec((unit, width), lambda i, order: (i, 0))],
        ),
        out_shape=[jax.ShapeDtypeStruct(shape, f32) for shape in shapes + [(4 * unit, width)]],
        compiler_params=pltpu.CompilerParams(vmem_limit_bytes=VMEM_LIMIT),
        cost_estimate=COST,
        name="give_pieces",
    )(quarter ^ jnp.arange(4), pieces)


def sum_kernel(left_at, late_at, y_at, left, right, late, left_came, right_came, late_came, *refs):
    to_y, kept_y, kept_x, to_x, scratch = refs
    dx, kind = pl.program_id(0), pl.program_id(1)
    half, shard, _ = to_y.shape[2:]
    lefts = jnp.concatenate([left[0], left_came[0]], axis=0)
    rights = jnp.concatenate([right[0], right_came[0]], axis=0)
    lates = jnp.concatenate([late[0], late_came[0]], axis=0)
    scratch[...] = left_dot(lefts, jnp.where(kind == 0, lates, rights))

    def rows_of(z, y):
        start = pl.multiple_of((2 * z + y) * shard, 8)
        return scratch[pl.ds(start, shard), :].astype(bf16)

    for z in range(half):
        to_y[0, 0, z] = rows_of(z, 1 - y_at[0])
        kept_y[0, 0, z] = rows_of(z, y_at[0])

    def write(out):
        for z in range(half):
            for y in range(2):
                out[0, z, y] = rows_of(half + z, y)

    @pl.when(dx == 0)
    def _():
        write(kept_x)

    @pl.when(dx == 1)
    def _():
        write(to_x)


def sum_blocks(early, late, early_came, late_came, quarter, at_y, z_size):
    _, rows, width = early.shape
    half, kinds = z_size // 2, 3
    shard = width // (2 * z_size)
    low = (2, kinds, half, shard, width)
    high = (kinds, half, 2, shard, width)
    low_spec = pl.BlockSpec((1, 1) + low[2:], lambda d, k, *_: (d, k, 0, 0, 0))
    block = (1, rows, width)
    quarters = jnp.stack([quarter, quarter ^ 2])
    left = pl.BlockSpec(
        block, lambda d, k, left, *_: (jnp.where(k == 0, left[d], jnp.where(k == 1, 2, 4 + d)), 0, 0)
    )
    right = pl.BlockSpec(block, lambda d, k, *_: (jnp.where(k == 2, 3, 6 + d), 0, 0))
    last = pl.BlockSpec(block, lambda d, k, left, late, y: (late[d], 0, 0))
    return pl.pallas_call(
        sum_kernel,
        grid_spec=pltpu.PrefetchScalarGridSpec(
            num_scalar_prefetch=3,
            grid=(2, kinds),
            in_specs=[left, right, last] * 2,
            out_specs=[
                low_spec,
                low_spec,
                pl.BlockSpec((1,) + high[1:], lambda d, k, *_: (jnp.where(d == 0, k, kinds - 1), 0, 0, 0, 0)),
                pl.BlockSpec((1,) + high[1:], lambda d, k, *_: (jnp.where(d == 1, k, 0), 0, 0, 0, 0)),
            ],
            scratch_shapes=[pltpu.VMEM((width, width), f32)],
        ),
        out_shape=[jax.ShapeDtypeStruct(shape, bf16) for shape in (low, low, high, high)],
        compiler_params=pltpu.CompilerParams(vmem_limit_bytes=VMEM_LIMIT),
        cost_estimate=COST,
        name="sum_blocks",
    )(
        jnp.where(quarters == 3, 1, 0),
        quarters,
        at_y.reshape(1),
        early,
        early,
        late,
        early_came,
        early_came,
        late_came,
    )


def pack_kernel(quarter_ref, weight, fc1_bias, *refs, unit):
    vectors, out = refs[:-1], refs[-1]
    lanes = out.shape[1]
    out[0 : weight.shape[0], :] = weight[...]
    row = weight.shape[0]
    fc1_rows = [fc1_bias[pl.ds(quarter_ref[0] ^ q, 1), :] for q in range(4)]
    pieces = [
        fc1_rows[q][:, i : i + unit] for i in range(0, fc1_bias.shape[1], unit) for q in range(4)
    ]
    for vector in [v[...] for v in vectors] + [jnp.concatenate(pieces, axis=1)]:
        for i in range(0, vector.shape[1], lanes):
            out[row : row + 1, :] = vector[:, i : i + lanes]
            row += 1
    out[row:, :] = jnp.zeros((out.shape[0] - row, lanes), f32)


def pack_small(weight, vectors, fc1_bias, unit, quarter):
    lanes = weight.shape[1]
    count = weight.shape[0] + (sum(v.shape[1] for v in vectors) + fc1_bias.size) // lanes
    shape = (-(-count // 8) * 8, lanes)
    whole = lambda i, at: (0, 0)
    arrays = (weight, fc1_bias, *vectors)
    return pl.pallas_call(
        functools.partial(pack_kernel, unit=unit),
        grid_spec=pltpu.PrefetchScalarGridSpec(
            num_scalar_prefetch=1,
            grid=(1,),
            in_specs=[pl.BlockSpec(array.shape, whole) for array in arrays],
            out_specs=pl.BlockSpec(shape, whole),
        ),
        out_shape=jax.ShapeDtypeStruct(shape, f32),
        compiler_params=pltpu.CompilerParams(vmem_limit_bytes=VMEM_LIMIT),
        cost_estimate=COST,
        name="pack_small",
    )(quarter.reshape(1), *arrays)


PAIR = [(0, 1), (1, 0)]
CORNER = [(i, i ^ 3) for i in range(4)]


def swap_core(value):
    return lax.ppermute(value, "c", PAIR)


def swap_x(value):
    return lax.ppermute(value, "x", PAIR)


def swap_y(value):
    return lax.ppermute(value, "y", PAIR)


def swap_plane(values):
    return [
        values[0],
        swap_y(values[1]),
        swap_x(values[2]),
        lax.ppermute(values[3], ("x", "y"), CORNER),
    ]


def after(values, *earlier):
    return lax.optimization_barrier((values, earlier))[0]


def pick(pieces, index):
    return lax.dynamic_index_in_dim(pieces, index, 0, keepdims=False)


UP, DOWN = ([(i, (i + step) % 4) for i in range(4)] for step in (1, 3))


def gather_z_start(own):
    if lax.axis_size("z") != 4:
        return (lax.all_gather(own, "z", axis=0, tiled=False),)
    return lax.ppermute(own, "z", UP), lax.ppermute(own, "z", DOWN)


def gather_z_end(own, came):
    at = lax.axis_index("z")
    if lax.axis_size("z") != 4:
        return came[0]
    half = own.shape[-2] // 2
    below, above = came
    across = [
        lax.ppermute(below[..., :half, :], "z", UP),
        lax.ppermute(above[..., half:, :], "z", DOWN),
    ]
    out = jnp.zeros((4,) + own.shape, own.dtype)
    for piece, step in ((own, 0), (below, 3), (above, 1), (jnp.concatenate(across, axis=-2), 2)):
        out = lax.dynamic_update_index_in_dim(out, piece, (at + step) % 4, 0)
    return out


def scatter_z(pieces):
    size, at = lax.axis_size("z"), lax.axis_index("z")
    if size != 4:
        return lax.psum_scatter(pieces, "z", scatter_dimension=0, tiled=False)
    half = pieces.shape[-2] // 2
    own, above, across, below = (pick(pieces, (at + step) % 4) for step in range(4))
    from_below = lax.ppermute(across[..., :half, :], "z", UP)
    from_above = lax.ppermute(across[..., half:, :], "z", DOWN)
    above = jnp.concatenate([add_low(above[..., :half, :], from_below), above[..., half:, :]], axis=-2)
    below = jnp.concatenate([below[..., :half, :], add_low(below[..., half:, :], from_above)], axis=-2)
    total = own.astype(f32) + lax.ppermute(above, "z", UP).astype(f32)
    return (total + lax.ppermute(below, "z", DOWN).astype(f32)).astype(bf16)


def gather_quarters(own):
    across = swap_x(own)
    return jnp.stack([own, swap_core(own), across, swap_core(across)])


def total_of(value, earlier):
    value = value + swap_core(value)
    value = value + swap_x(value)
    value = value + swap_y(value)
    value = after(value, earlier)
    size, step = lax.axis_size("z"), 1
    while step < size:
        value = value + lax.ppermute(value, "z", [(i, i ^ step) for i in range(size)])
        step *= 2
    return value


def add_low(left, right):
    return (left.astype(f32) + right.astype(f32)).astype(bf16)


def join_y(own, other):
    at_y = lax.axis_index("y")
    both = [jnp.where(at_y == 0, own, other), jnp.where(at_y == 0, other, own)]
    return jnp.stack(both, axis=1).reshape(-1, own.shape[-1])


def gather_start(column):
    half = column.shape[0] // 2
    return swap_y(column[:half]), swap_x(column[half:])


def gather_more(column, came):
    half, kinds = column.shape[0] // 2, column.shape[1]
    low = jnp.stack([join_y(column[:half, kind], came[0][:, kind]) for kind in range(kinds)])
    high = jnp.stack([column[half:], came[1]])
    return low, high


def gather_end(low, high, low_x, high_y):
    return [
        [
            jnp.concatenate([from_low[kind], join_y(high[dx][:, kind], high_y[dx][:, kind])])
            for dx, from_low in enumerate((low, low_x))
        ]
        for kind in range(low.shape[0])
    ]


def sum_more(kept_y, kept_x, from_y, from_x, at_y):
    low = [add_low(kept_y[dx], from_y[dx]) for dx in range(2)]
    high = [
        add_low(*(lax.dynamic_index_in_dim(v, y, 2, False) for v in (kept_x, from_x))) for y in (at_y, 1 - at_y)
    ]
    return low[0], high[0], low[1], high[1]


def sum_end(low, high, low_x, high_y):
    return jnp.concatenate([add_low(low, low_x), add_low(high, high_y)], axis=1).swapaxes(0, 1)


def body(
    pixels,
    wave_table,
    wave_weight,
    wave_bias,
    gen_weight,
    patch_bias,
    norm1_gain,
    norm1_bias,
    qkv_weight,
    query_bias,
    value_bias,
    out_weight,
    out_bias,
    norm2_gain,
    norm2_bias,
    fc1_weight,
    fc1_bias,
    fc2_weight,
    fc2_bias,
    band_count,
    band_table,
    cotangent,
):
    tile_count, seq_len, band_slots, pixel_count = pixels.shape[1:]
    model_width = gen_weight.shape[1]
    wave_width = wave_weight.shape[0]
    hidden_width = fc1_weight.shape[1]
    head_size = model_width // HEADS
    score_scale = head_size ** (-0.5)
    row_count = tile_count * seq_len
    head_shape = (tile_count, seq_len, HEADS, head_size)
    z_size = lax.axis_size("z")
    row_size = 2 * z_size
    at_x, at_c, at_y = lax.axis_index("x"), lax.axis_index("c"), lax.axis_index("y")
    quarter = 2 * at_x + at_c
    shard = qkv_weight.shape[0]
    unit = hidden_width // row_size // 4

    gen_rows = gen_weight.shape[0] // 4
    own_rows = lax.dynamic_slice_in_dim(gen_weight, quarter * gen_rows, gen_rows, 0)
    gen = lax.all_gather(own_rows, ("c", "z"), axis=0, tiled=True).reshape(-1, pixel_count, model_width)

    unit_order = fc1_bias.reshape(row_size, 4, unit).transpose(1, 0, 2).reshape(4, row_size * unit)
    bias_fc1 = [pick(unit_order, quarter ^ d) for d in range(4)]

    onehot = (band_table[0][:, None] == jnp.arange(wave_table.shape[0])[None, :]).astype(f32)
    wavelength = jnp.dot(onehot, wave_table, precision=highest)
    wave_embed = sincos(wavelength * 1000.0, wave_width)
    live = (jnp.arange(band_slots) < band_count[0]).astype(f32)[:, None]

    def hyper_fn(weight, bias):
        return jax.nn.gelu(jnp.dot(wave_embed, weight, precision=highest) + bias) * live

    hyper, hyper_back = jax.vjp(hyper_fn, wave_weight.astype(f32), wave_bias)
    per_row = wave_width // row_size
    place = jnp.arange(wave_width)
    kk = place % (per_row // 4)
    place = place // (per_row // 4)
    entry_z = place % z_size
    place = place // z_size
    entry_c, entry_y, entry_x = place % 2, (place // 2 % 2) ^ at_y, (place // 4) ^ at_x
    entry = per_row * (2 * entry_z + entry_y) + per_row // 4 * (2 * entry_x + entry_c) + kk
    order = (jnp.arange(wave_width)[:, None] == entry[None, :]).astype(bf16)
    hyper_low = dense_dot(hyper.astype(bf16), order).astype(bf16)

    pixel_rows = pixels.reshape(row_count, band_slots, pixel_count).transpose(1, 0, 2)
    mixed_pixels = mix_pixels(hyper_low.T, pixel_rows)
    patches = swap_plane(mixed_pixels)

    weights = after((qkv_weight, out_weight, fc1_weight, fc2_weight), mixed_pixels)
    own_pieces = take_pieces(*weights, quarter)
    column = gather_z_end(own_pieces, gather_z_start(own_pieces))
    column, patches = after((column, patches))
    column_came = gather_start(column)
    low, high = gather_more(column, column_came)
    attn, fc = (low[:1], high[:, :, :1]), (low[1:], high[:, :, 1:])
    attn_came = swap_x(attn[0]), swap_y(attn[1])
    attn_came, fc = after((attn_came, fc))
    fc_came = swap_x(fc[0]), swap_y(fc[1])

    def both_cores(blocks):
        return [block for owned in blocks for block in (owned, swap_core(owned))]

    attn = jnp.stack(both_cores(gather_end(*attn, *attn_came)[0]))
    gen = after(gen, attn_came)
    partial = project(patches, gen)
    partial = [partial[j * row_count : (j + 1) * row_count] for j in range(4)]
    partial = [partial[0]] + swap_plane([piece.astype(bf16) for piece in partial])[1:]
    projected = (partial[0] + partial[1]) + (partial[2] + partial[3])
    fc_came = after(fc_came, projected)
    w_query, w_key, w_value, w_out = (pick(attn, j ^ quarter) for j in range(4))
    position = sincos(jnp.arange(seq_len).astype(f32), model_width)
    embedded = (projected + patch_bias).reshape(tile_count, seq_len, model_width) + position
    embedded = embedded.reshape(row_count, model_width)

    normed = layer_norm(embedded, norm1_gain, norm1_bias).astype(bf16)
    queries = (dense_dot(normed, w_query) + query_bias).astype(bf16).reshape(head_shape)
    key_rows = dense_dot(normed, w_key).astype(bf16).reshape(head_shape)
    value_rows = (dense_dot(normed, w_value) + value_bias).astype(bf16).reshape(head_shape)
    scores = (
        jnp.einsum("tqhd,tkhd->thqk", queries, key_rows, preferred_element_type=f32) * score_scale
    )
    probs_full = jax.nn.softmax(scores, axis=-1)
    probs = probs_full.astype(bf16)
    attended = (
        jnp.einsum("thqk,tkhd->tqhd", probs, value_rows, preferred_element_type=f32)
        .astype(bf16)
        .reshape(row_count, model_width)
    )
    middle = embedded + dense_dot(attended, w_out) + out_bias
    fc_came = after(fc_came, middle)
    w_fc1, w_fc2 = (both_cores(blocks) for blocks in gather_end(*fc, *fc_came))
    other_patches = [swap_core(part) for part in after(patches, middle)]
    normed_two = layer_norm(middle, norm2_gain, norm2_bias).astype(bf16)
    fc_pre = [dense_dot(normed_two, w) + bias for w, bias in zip(w_fc1, bias_fc1)]
    hidden, gelu_back = zip(*(jax.vjp(jax.nn.gelu, values) for values in fc_pre))
    hidden = [values.astype(bf16) for values in hidden]
    block_out = middle + sum(dense_dot(values, w) for values, w in zip(hidden, w_fc2)) + fc2_bias

    grad_out = cotangent.reshape(row_count, model_width)
    fc2_bias_part = row_total(grad_out)
    grad_pre = [
        back(right_dot(grad_out, w))[0].astype(bf16) for back, w in zip(gelu_back, w_fc2)
    ]
    fc1_bias_part = jnp.concatenate([row_total(values) for values in grad_pre])
    common = [normed, attended, normed_two, grad_out]
    early_values = jnp.stack(common + [hidden[0], hidden[2], grad_pre[0], grad_pre[2]])
    early_came = swap_core(jnp.stack(common + [hidden[1], hidden[3], grad_pre[1], grad_pre[3]]))
    grad_normed_two = sum(right_dot(values, w) for values, w in zip(grad_pre, w_fc1))
    norm_two_back = jax.vjp(layer_norm, middle, norm2_gain, norm2_bias)[1]
    grad_middle, norm2_gain_part, norm2_bias_part = norm_two_back(grad_normed_two)
    grad_middle = grad_middle + grad_out.astype(f32)
    grad_branch = grad_middle.astype(bf16)
    out_bias_part = row_total(grad_branch)
    grad_attended = right_dot(grad_branch, w_out).astype(bf16).reshape(head_shape)
    grad_probs = jnp.einsum(
        "tqhd,tkhd->thqk", grad_attended, value_rows, preferred_element_type=f32
    )
    grad_scores = probs_full * (
        grad_probs - jnp.sum(probs_full * grad_probs, axis=-1, keepdims=True)
    )
    grad_scores = grad_scores.astype(bf16)
    grad_queries = (
        jnp.einsum("thqk,tkhd->tqhd", grad_scores, key_rows, preferred_element_type=f32)
        * score_scale
    ).astype(bf16)
    grad_keys = (
        jnp.einsum("thqk,tqhd->tkhd", grad_scores, queries, preferred_element_type=f32)
        * score_scale
    ).astype(bf16)
    grad_values = jnp.einsum(
        "thqk,tqhd->tkhd", probs, grad_attended, preferred_element_type=f32
    ).astype(bf16)
    grad_queries = grad_queries.reshape(row_count, model_width)
    grad_values = grad_values.reshape(row_count, model_width)
    grad_keys = grad_keys.reshape(row_count, model_width)
    query_bias_part = row_total(grad_queries)
    value_bias_part = row_total(grad_values)
    grad_normed = right_dot(grad_queries, w_query)
    grad_normed += right_dot(grad_keys, w_key)
    grad_normed += right_dot(grad_values, w_value)
    grad_normed, early_came, other_patches = after((grad_normed, early_came, other_patches))
    norm_one_back = jax.vjp(layer_norm, embedded, norm1_gain, norm1_bias)[1]
    grad_from_norm, norm1_gain_part, norm1_bias_part = norm_one_back(grad_normed)
    grad_embedded = (grad_middle + grad_from_norm).astype(bf16)
    patch_bias_part = row_total(grad_embedded)

    grads = swap_plane([grad_embedded] * 4)
    early = early_rows(row_count)
    back_early = back_patches(grads, gen, 0, early)
    grads, back_early = after((grads, back_early))
    back_early = swap_plane(back_early)
    other_grads = swap_core(jnp.concatenate(grads))
    chunks = 2 if wave_width // row_size // 4 == GEN_STEP else 1
    gen_sent = gen_grad(patches, other_patches, grads, other_grads, chunks, at_c)
    gen_parts = [
        lax.psum_scatter(chunk.reshape(-1, model_width), "z", scatter_dimension=0, tiled=True)
        for chunk in gen_sent
    ]

    late_values = jnp.stack([grad_queries, grad_keys, grad_values, grad_branch])
    late_came = swap_core(late_values)
    to_y, kept_y, kept_x, to_x = sum_blocks(
        early_values, late_values, early_came, late_came, quarter, at_y, z_size
    )
    back_late = back_patches(after(grads, gen_sent), gen, early, row_count - early)
    to_y, to_x, back_early, back_late = after((to_y, to_x, back_early, back_late))
    back_late = swap_plane(back_late)
    from_y, from_x = swap_y(to_y), swap_x(to_x)
    pixel_grad, hyper_early = pixel_back(hyper_low, pixel_rows, back_early, 0)
    back_late, from_y, from_x, hyper_early = after((back_late, from_y, from_x, hyper_early))
    low, high, low_sent, high_sent = sum_more(kept_y, kept_x, from_y, from_x, at_y)
    low_x, high_y = swap_x(low_sent), swap_y(high_sent)
    pixel_grad, hyper_late = pixel_back(hyper_low, pixel_rows, back_late, early, (pixel_grad,))
    low_x, high_y, hyper_late, gen_parts = after((low_x, high_y, hyper_late, gen_parts))
    across = [swap_x(piece) for piece in gen_parts]
    gen_total = ()
    for chunk, piece in enumerate(gen_parts):
        pair = piece, swap_core(piece)
        gen_total = (put_parts(pair, (quarter, quarter ^ 1), chunk, chunks, gen_total),)
    share_sum = scatter_z(sum_end(low, high, low_x, high_y))
    qkv_total, out_total, fc1_total, fc2_total = give_pieces(gather_quarters(share_sum), quarter, hidden_width)

    grad_hyper = hyper_early + hyper_late
    grad_hyper = lax.dot_general(
        grad_hyper, order.astype(f32), (((1,), (1,)), ((), ())), precision=highest
    )
    wave_weight_part, wave_bias_part = hyper_back(grad_hyper)
    norm_parts = [norm1_gain_part, norm1_bias_part, norm2_gain_part, norm2_bias_part, wave_bias_part]
    norm_parts = [part.reshape(1, -1) for part in norm_parts]
    small = [*norm_parts, patch_bias_part, query_bias_part, value_bias_part, out_bias_part, fc2_bias_part]
    cuts = np.cumsum([part.shape[1] for part in small] + [hidden_width])
    small = pack_small(wave_weight_part, small, fc1_bias_part, unit, quarter)
    small = total_of(small, (share_sum, gen_total))
    for chunk, piece in enumerate(across):
        pair = piece, swap_core(piece)
        gen_total = (put_parts(pair, (quarter ^ 2, quarter ^ 3), chunk, chunks, gen_total),)
    gen_total = gen_total[0]
    wave_weight_total, small = small[:wave_width], small[wave_width:].reshape(-1)
    (
        norm1_gain_total,
        norm1_bias_total,
        norm2_gain_total,
        norm2_bias_total,
        wave_bias_total,
        patch_bias_total,
        query_bias_total,
        value_bias_total,
        out_bias_total,
        fc2_bias_total,
        fc1_bias_total,
        _,
    ) = jnp.split(small, cuts)
    block_result = block_out.astype(bf16).reshape(1, tile_count, seq_len, model_width)
    pixel_result = pixel_grad.transpose(1, 0, 2).reshape(1, tile_count, seq_len, band_slots, pixel_count)
    return (
        block_result,
        pixel_result,
        wave_weight_total,
        wave_bias_total,
        gen_total,
        patch_bias_total,
        norm1_gain_total,
        norm1_bias_total,
        qkv_total,
        query_bias_total,
        value_bias_total,
        out_total,
        out_bias_total,
        norm2_gain_total,
        norm2_bias_total,
        fc1_total,
        fc1_bias_total,
        fc2_total,
        fc2_bias_total,
    )


def row_sum(values):
    return jnp.sum(values.astype(f32), axis=0)


def general_body(
    pixels,
    wave_table,
    wave_weight,
    wave_bias,
    gen_weight,
    patch_bias,
    norm1_gain,
    norm1_bias,
    qkv_weight,
    query_bias,
    value_bias,
    out_weight,
    out_bias,
    norm2_gain,
    norm2_bias,
    fc1_weight,
    fc1_bias,
    fc2_weight,
    fc2_bias,
    band_count,
    band_table,
    cotangent,
):
    tile_count, seq_len, band_slots, pixel_count = pixels.shape[1:]
    model_width = gen_weight.shape[1]
    wave_width = wave_weight.shape[0]
    head_size = model_width // HEADS
    score_scale = head_size ** (-0.5)
    row_count = tile_count * seq_len
    head_shape = (tile_count, seq_len, HEADS, head_size)
    pixel_rows = pixels.reshape(row_count, band_slots, pixel_count)
    onehot = (band_table[0][:, None] == jnp.arange(wave_table.shape[0])[None, :]).astype(
        f32
    )
    wavelength = jnp.dot(onehot, wave_table, precision=highest)
    wave_embed = sincos(wavelength * 1000.0, wave_width)
    live = (jnp.arange(band_slots) < band_count[0]).astype(f32)[:, None]

    def hyper_fn(weight, bias):
        return jax.nn.gelu(jnp.dot(wave_embed, weight, precision=highest) + bias) * live

    hyper, hyper_back = jax.vjp(hyper_fn, wave_weight.astype(f32), wave_bias)
    hyper_low = hyper.astype(bf16)
    patches = jnp.einsum("bk,rbp->rkp", hyper_low, pixel_rows, preferred_element_type=f32)
    patches = patches.astype(bf16).reshape(row_count, wave_width * pixel_count)
    position = sincos(jnp.arange(seq_len).astype(f32), model_width)
    columns = patches
    projected = dense_dot(columns, lax.all_gather(gen_weight, "row", axis=0, tiled=True))
    embedded = (projected + patch_bias).reshape(tile_count, seq_len, model_width) + position
    embedded = embedded.reshape(row_count, model_width)
    w_qkv, w_out, w_fc1, w_fc2 = (
        lax.all_gather(qkv_weight, "row", axis=0, tiled=True),
        lax.all_gather(out_weight, "row", axis=0, tiled=True),
        lax.all_gather(fc1_weight, "row", axis=0, tiled=True),
        lax.all_gather(fc2_weight, "row", axis=0, tiled=True),
    )

    def front(inputs):
        normed = layer_norm(inputs, norm1_gain, norm1_bias).astype(bf16)
        mixed = dense_dot(normed, w_qkv)
        queries = (mixed[:, :model_width] + query_bias).astype(bf16).reshape(head_shape)
        key_rows = mixed[:, model_width : 2 * model_width].astype(bf16).reshape(head_shape)
        value_rows = (
            (mixed[:, 2 * model_width :] + value_bias).astype(bf16).reshape(head_shape)
        )
        return (normed, queries, key_rows, value_rows)

    def scores_of(queries, key_rows):
        return (
            jnp.einsum("tqhd,tkhd->thqk", queries, key_rows, preferred_element_type=f32)
            * score_scale
        )

    def attend(probs, value_rows):
        mixed_heads = jnp.einsum(
            "thqk,tkhd->tqhd", probs, value_rows, preferred_element_type=f32
        )
        return mixed_heads.astype(bf16).reshape(row_count, model_width)

    def back_half(inputs, attended):
        middle = inputs + dense_dot(attended, w_out) + out_bias
        normed_two = layer_norm(middle, norm2_gain, norm2_bias).astype(bf16)
        fc_pre = dense_dot(normed_two, w_fc1) + fc1_bias
        hidden = jax.nn.gelu(fc_pre).astype(bf16)
        return (middle, normed_two, fc_pre, hidden)

    normed, queries, key_rows, value_rows = front(embedded)
    scores = scores_of(queries, key_rows)
    log_total = jax.nn.logsumexp(scores, axis=-1, keepdims=True)
    attended = attend(jnp.exp(scores - log_total).astype(bf16), value_rows)
    middle, normed_two, fc_pre, hidden = back_half(embedded, attended)
    block_out = middle + dense_dot(hidden, w_fc2) + fc2_bias
    grad_out = cotangent.reshape(row_count, model_width)
    normed, queries, key_rows, value_rows = front(embedded)
    probs_full = jnp.exp(scores_of(queries, key_rows) - log_total)
    probs = probs_full.astype(bf16)
    attended = attend(probs, value_rows)
    middle, normed_two, fc_pre, hidden = back_half(embedded, attended)
    fc2_bias_part = row_sum(grad_out)
    fc2_grad = left_dot(hidden, grad_out)
    grad_hidden = right_dot(grad_out, w_fc2)
    grad_pre = jax.vjp(jax.nn.gelu, fc_pre)[1](grad_hidden)[0].astype(bf16)
    fc1_bias_part = row_sum(grad_pre)
    fc1_grad = left_dot(normed_two, grad_pre)
    grad_normed_two = right_dot(grad_pre, w_fc1)
    norm_two_back = jax.vjp(layer_norm, middle, norm2_gain, norm2_bias)[1]
    grad_middle, norm2_gain_part, norm2_bias_part = norm_two_back(grad_normed_two)
    grad_middle = grad_middle + grad_out.astype(f32)
    grad_branch = grad_middle.astype(bf16)
    out_bias_part = row_sum(grad_branch)
    out_grad = left_dot(attended, grad_branch)
    grad_attended = right_dot(grad_branch, w_out).astype(bf16).reshape(head_shape)
    grad_probs = jnp.einsum(
        "tqhd,tkhd->thqk", grad_attended, value_rows, preferred_element_type=f32
    )
    grad_scores = probs_full * (
        grad_probs - jnp.sum(probs_full * grad_probs, axis=-1, keepdims=True)
    )
    grad_scores = grad_scores.astype(bf16)
    grad_queries = (
        jnp.einsum("thqk,tkhd->tqhd", grad_scores, key_rows, preferred_element_type=f32)
        * score_scale
    ).astype(bf16)
    grad_keys = (
        jnp.einsum("thqk,tqhd->tkhd", grad_scores, queries, preferred_element_type=f32)
        * score_scale
    ).astype(bf16)
    grad_values = jnp.einsum(
        "thqk,tqhd->tkhd", probs, grad_attended, preferred_element_type=f32
    ).astype(bf16)
    grad_queries = grad_queries.reshape(row_count, model_width)
    grad_values = grad_values.reshape(row_count, model_width)
    grad_mixed = jnp.concatenate(
        [grad_queries, grad_keys.reshape(row_count, model_width), grad_values], axis=1
    )
    query_bias_part = row_sum(grad_queries)
    value_bias_part = row_sum(grad_values)
    qkv_grad = left_dot(normed, grad_mixed)
    grad_normed = right_dot(grad_mixed, w_qkv)
    norm_one_back = jax.vjp(layer_norm, embedded, norm1_gain, norm1_bias)[1]
    grad_from_norm, norm1_gain_part, norm1_bias_part = norm_one_back(grad_normed)
    grad_embedded = (grad_middle + grad_from_norm).astype(bf16)
    patch_bias_part = row_sum(grad_embedded)
    grad_patches = right_dot(
        grad_embedded, lax.all_gather(gen_weight, "row", axis=0, tiled=True)
    ).astype(bf16)
    grad_cube = grad_patches.reshape(row_count, wave_width, pixel_count)
    pixel_grad = jnp.einsum(
        "rkp,bk->rbp", grad_cube, hyper_low, preferred_element_type=f32
    ).astype(bf16)
    grad_hyper = jnp.einsum(
        "rkp,rbp->bk", grad_cube, pixel_rows, preferred_element_type=f32
    )
    wave_weight_part, wave_bias_part = hyper_back(grad_hyper)
    columns = patches
    gen_part = lax.psum_scatter(
        left_dot(columns, grad_embedded), "row", scatter_dimension=0, tiled=True
    )
    qkv_share, out_share, fc1_share, fc2_share = (
        lax.psum_scatter(qkv_grad, "row", scatter_dimension=0, tiled=True),
        lax.psum_scatter(out_grad, "row", scatter_dimension=0, tiled=True),
        lax.psum_scatter(fc1_grad, "row", scatter_dimension=0, tiled=True),
        lax.psum_scatter(fc2_grad, "row", scatter_dimension=0, tiled=True),
    )
    gen_total, qkv_total, out_total, fc1_total, fc2_total = (
        lax.psum(gen_part.astype(bf16), "grp").astype(f32),
        lax.psum(qkv_share.astype(bf16), "grp").astype(f32),
        lax.psum(out_share.astype(bf16), "grp").astype(f32),
        lax.psum(fc1_share.astype(bf16), "grp").astype(f32),
        lax.psum(fc2_share.astype(bf16), "grp").astype(f32),
    )
    small_totals = lax.psum(
        (
            wave_weight_part,
            wave_bias_part,
            patch_bias_part,
            norm1_gain_part,
            norm1_bias_part,
            query_bias_part,
            value_bias_part,
            out_bias_part,
            norm2_gain_part,
            norm2_bias_part,
            fc1_bias_part,
            fc2_bias_part,
        ),
        ("grp", "row"),
    )
    (
        wave_weight_total,
        wave_bias_total,
        patch_bias_total,
        norm1_gain_total,
        norm1_bias_total,
        query_bias_total,
        value_bias_total,
        out_bias_total,
        norm2_gain_total,
        norm2_bias_total,
        fc1_bias_total,
        fc2_bias_total,
    ) = small_totals
    block_result = block_out.astype(bf16).reshape(1, tile_count, seq_len, model_width)
    pixel_result = pixel_grad.reshape(1, tile_count, seq_len, band_slots, pixel_count)
    return (
        block_result,
        pixel_result,
        wave_weight_total,
        wave_bias_total,
        gen_total,
        patch_bias_total,
        norm1_gain_total,
        norm1_bias_total,
        qkv_total,
        query_bias_total,
        value_bias_total,
        out_total,
        out_bias_total,
        norm2_gain_total,
        norm2_bias_total,
        fc1_total,
        fc1_bias_total,
        fc2_total,
        fc2_bias_total,
    )


def solution(mesh):
    grp_size, row_size = mesh.devices.shape
    if (grp_size, row_size) == PLANNED:
        step, grp, row = body, ("x", "c"), ("z", "y")
        mesh = Mesh(mesh.devices.reshape(grp_size // 2, 2, row_size // 2, 2), AXES)
    else:
        step, grp, row = general_body, "grp", "row"
    return jax.shard_map(
        step,
        mesh=mesh,
        in_specs=(
            P(grp, row, None, None, None),
            P(),
            P(),
            P(),
            P(row, None),
            P(),
            P(),
            P(),
            P(row, None),
            P(),
            P(),
            P(row, None),
            P(),
            P(),
            P(),
            P(row, None),
            P(),
            P(row, None),
            P(),
            P(grp),
            P(grp, None),
            P(grp, row, None, None),
        ),
        out_specs=(
            P(grp, row, None, None),
            P(grp, row, None, None, None),
            P(),
            P(),
            P(row, None),
            P(),
            P(),
            P(),
            P(row, None),
            P(),
            P(),
            P(row, None),
            P(),
            P(),
            P(),
            P(row, None),
            P(),
            P(row, None),
            P(),
        ),
        check_vma=False,
    )
```
